128 devices in a mesh: feat: 4 (over y), dom: 32 (over x, z, core).
Axes of the slice: x: 4, y: 4, z: 4, core: 2. Of those that a mesh axis runs over, the one named last changes fastest.
Arguments:
- features: bfloat16 [4, 32, 512, 1024], P(None, 'dom', None, 'feat'), may hold values from -100 to 100
- w_self: bfloat16 [1024, 256], P('feat'), may hold values from -0.1875 to 0.1875
- w_neigh: bfloat16 [1024, 256], P('feat'), may hold values from -2 to 2
- gain: float32 [256], replicated, may hold values from 0.5 to 1.5
- shift: float32 [256], replicated, may hold values from -1 to 1
- d_hidden: bfloat16 [4, 32, 512, 256], P('feat', 'dom'), may hold values from -32 to 32
- send_rows: int32 [4, 32, 128, 32], P('feat', 'dom'), may hold values from 0 to 511
- send_count: int32 [4, 32, 128], P('feat', 'dom'), may hold values from 0 to 32, as said below
- tile_src: int32 [4, 32, 160], P('feat', 'dom'), may hold values from 0 to 35, as said below
- tile_dst: int32 [4, 32, 160], P('feat', 'dom'), may hold values from 0 to 3
- tile_count: int32 [4, 32], P('feat', 'dom'), may hold values from 36 to 160, as said below
- tile_vals: bfloat16 [4, 32, 160, 128, 128], P('feat', 'dom'), may hold values from 0 to 1, as said below
Outputs:
- hidden: bfloat16 [4, 32, 512, 256], P('feat', 'dom')
- d_self: bfloat16 [4, 32, 512, 256], P('feat', 'dom')
- d_neigh: bfloat16 [4, 32, 512, 256], P('feat', 'dom')
- gain_grad: float32 [256], replicated
- shift_grad: float32 [256], replicated
The draws below stay inside these ranges and needn't reach their ends.
Inputs may be any that keep to these rules, and one draw needn't show every extreme that they name: `send_rows`: rows may repeat within a list. `send_count`: the live slots are the first ones; in every draw some receiving partition gets 32 live slots from every partition. `tile_src`: blocks below 4 are the partition's own nodes, the others the halo rows in order of sender and slot; the first 36 tiles of each partition name every source block once. `tile_count`: the live tiles are the first ones; some partition has all 160 live. `tile_vals`: nonnegative; tiles past a partition's count are not used.
All inputs are finite; a program needn't handle non-finite values.
Results may differ from the reference program's by a relative error of at most 0.0056.
Values may be sent and summed in bfloat16 or wider, within the bound.
No kernel may reach another device: no remote copies, remote signals or barrier semaphores. Data moves between devices by JAX's collectives and lax.ppermute only.
A program may use at most 64 MiB of HBM per device.

```python
import jax
import jax.numpy as jnp
from jax import lax

F = 1024
HID = 256
TILE = 128
ROWS_DEV = 512
SLOTS = 32
FGROUPS = 4
DGROUPS = 32
PARTS_SIZE = 128
NODES = 65536
LOCAL_BLOCKS = 4
HALO_ROWS = 4096
SRC_BLOCKS = 36
TILES = 160


def partition_ramp():
    position = jnp.arange(FGROUPS)[:, None] * DGROUPS + jnp.arange(DGROUPS)[None, :]
    return (3.0 ** (position.astype(jnp.float32) / (PARTS_SIZE - 1)))[:, :, None, None]


def draw_features(key, part):
    subkeys = jax.random.split(jax.random.fold_in(key, 101), 3)
    full_shape = (FGROUPS, DGROUPS, ROWS_DEV, F)
    row_scale = jnp.exp(jax.random.uniform(subkeys[1], (FGROUPS, DGROUPS, ROWS_DEV, 1), minval=0.0, maxval=jnp.log(10.0)))
    col_scale = jnp.exp(jax.random.uniform(subkeys[2], (F,), minval=0.0, maxval=jnp.log(10.0)))
    noise = jax.random.truncated_normal(subkeys[0], -4.0, 4.0, full_shape)
    result = noise * row_scale * col_scale * partition_ramp() / 30.0
    return jnp.clip(result, -100.0, 100.0).astype(jnp.bfloat16)


def draw_d_hidden(key, part):
    subkeys = jax.random.split(jax.random.fold_in(key, 202), 3)
    full_shape = (FGROUPS, DGROUPS, ROWS_DEV, HID)
    column_bias = jax.random.uniform(subkeys[1], (HID,), minval=-1.0, maxval=1.0)
    row_scale = jnp.exp(jax.random.uniform(subkeys[2], (FGROUPS, DGROUPS, ROWS_DEV, 1), minval=0.0, maxval=jnp.log(4.0)))
    noise = jax.random.truncated_normal(subkeys[0], -4.0, 4.0, full_shape)
    result = (column_bias + noise) * row_scale * partition_ramp() / 2.0
    return jnp.clip(result, -32.0, 32.0).astype(jnp.bfloat16)


def draw_send_count(key, part):
    subkeys = jax.random.split(jax.random.fold_in(key, 303), 2)
    counts = jax.random.randint(subkeys[0], (FGROUPS, DGROUPS, PARTS_SIZE), 0, SLOTS + 1)
    busiest = jax.random.randint(subkeys[1], (), 0, PARTS_SIZE)
    counts = jnp.where(jnp.arange(PARTS_SIZE)[None, None, :] == busiest, SLOTS, counts)
    return counts.astype(jnp.int32)


def one_order(subkey):
    return jax.random.permutation(subkey, SRC_BLOCKS)


def draw_tile_src(key, part):
    subkeys = jax.random.split(jax.random.fold_in(key, 404), 2)
    orders = jax.vmap(one_order)(jax.random.split(subkeys[0], PARTS_SIZE))
    others = jax.random.randint(subkeys[1], (PARTS_SIZE, TILES - SRC_BLOCKS), 0, SRC_BLOCKS)
    return jnp.concatenate([orders.astype(jnp.int32), others.astype(jnp.int32)], axis=1).reshape(FGROUPS, DGROUPS, TILES)


def draw_tile_count(key, part):
    subkeys = jax.random.split(jax.random.fold_in(key, 505), 2)
    room = TILES - SRC_BLOCKS
    picks = jax.random.randint(subkeys[0], (PARTS_SIZE,), 0, room + 1)
    extra = picks * picks // max(room, 1)
    busiest = jax.random.randint(subkeys[1], (), 0, PARTS_SIZE)
    extra = jnp.where(jnp.arange(PARTS_SIZE) == busiest, room, extra)
    return (SRC_BLOCKS + extra).reshape(FGROUPS, DGROUPS).astype(jnp.int32)


def draw_tile_vals(key, part):
    subkeys = jax.random.split(jax.random.fold_in(key, 606), 2)
    full_shape = (FGROUPS, DGROUPS, TILES, TILE, TILE)
    present = jax.random.uniform(subkeys[0], full_shape) < 0.0625
    weights = jax.random.uniform(subkeys[1], full_shape, minval=0.25, maxval=1.0)
    return jnp.where(present, weights, 0.0).astype(jnp.bfloat16)


def set_ends(values, key, smallest, top_value):
    extent = values.shape
    spot = [jax.random.randint(jax.random.fold_in(key, axis), (), 0, extent[axis]) for axis in range(len(extent))]
    values = values.at[tuple(spot)].set(smallest)
    longest = extent.index(max(extent))
    spot[longest] = (spot[longest] + 1) % extent[longest]
    return values.at[tuple(spot)].set(top_value)


def shard_levels(rng, dims, shards, smallest, high):
    loudness, own = 1.0, jax.random.fold_in(rng, 6)
    for axis_at, parts in shards:
        steps = jnp.exp(jax.random.uniform(jax.random.fold_in(own, axis_at), (parts,), jnp.float32, smallest / len(shards), high / len(shards)))
        loudness = loudness * jnp.repeat(steps, dims[axis_at] // parts).reshape([-1 if axis == axis_at else 1 for axis in range(len(dims))])
    return loudness


def bell_draw(stream_key, dims, width, limit, pieces=(), held_as=jnp.bfloat16):
    values = jax.random.normal(stream_key, dims, jnp.float32) * width
    if len(pieces) > 0:
        values = shard_levels(stream_key, dims, pieces, -0.22, 0.18) * values
    return jnp.clip(values, min=-limit, max=limit).astype(held_as)


def setup_inputs(seed: int = 0) -> dict:
    key_list = jax.random.split(jax.random.key(seed), 13)
    return {
        "features": draw_features(jax.random.fold_in(key_list[12], 71), 0),
        "w_self": bell_draw(key_list[1], (F, HID), F ** -0.5, 0.1875, ((0, 4),)),
        "w_neigh": bell_draw(key_list[2], (F, HID), (max(F // 128, 1)) ** -0.5, 2.0, ((0, 4),)),
        "gain": jnp.clip(1.0 + 0.1 * jax.random.normal(key_list[3], (HID,), jnp.float32), 0.5, 1.5),
        "shift": jnp.clip(jax.random.uniform(key_list[4], (HID,), jnp.float32, -1.0, 1.0), -1.0, 1.0),
        "d_hidden": draw_d_hidden(jax.random.fold_in(key_list[12], 71), 0),
        "send_rows": set_ends(jax.random.randint(key_list[6], (FGROUPS, DGROUPS, PARTS_SIZE, SLOTS), 0, ROWS_DEV), jax.random.fold_in(key_list[6], 1), 0, ROWS_DEV - 1).astype(jnp.int32),
        "send_count": draw_send_count(jax.random.fold_in(key_list[12], 71), 0),
        "tile_src": draw_tile_src(jax.random.fold_in(key_list[12], 71), 0),
        "tile_dst": set_ends(jax.random.randint(key_list[9], (FGROUPS, DGROUPS, TILES), 0, LOCAL_BLOCKS), jax.random.fold_in(key_list[9], 1), 0, LOCAL_BLOCKS - 1).astype(jnp.int32),
        "tile_count": draw_tile_count(jax.random.fold_in(key_list[12], 71), 0),
        "tile_vals": draw_tile_vals(jax.random.fold_in(key_list[12], 71), 0),
    }


epsilon = 1e-05
highest = lax.Precision.HIGHEST

def reference(features, w_self, w_neigh, gain, shift, d_hidden, send_rows, send_count, tile_src, tile_dst, tile_count, tile_vals):
    stacked = features.reshape(NODES, F)
    own = jnp.dot(stacked, w_self, preferred_element_type=jnp.float32)
    neigh = jnp.dot(stacked, w_neigh, preferred_element_type=jnp.float32).astype(jnp.bfloat16).reshape(PARTS_SIZE, ROWS_DEV, HID)
    targets = send_rows.reshape(PARTS_SIZE, PARTS_SIZE, SLOTS)
    counts = send_count.reshape(PARTS_SIZE, PARTS_SIZE)
    live_slot = jnp.arange(SLOTS, dtype=jnp.int32)[None, None, :] < counts[:, :, None]
    tile_from = tile_src.reshape(PARTS_SIZE, TILES)
    tile_into = tile_dst.reshape(PARTS_SIZE, TILES)
    live_tiles = tile_count.reshape(PARTS_SIZE)
    values = tile_vals.reshape(PARTS_SIZE, TILES, TILE, TILE)
    senders = jnp.arange(PARTS_SIZE, dtype=jnp.int32)

    def aggregate(target):
        picked = neigh[senders[:, None], targets[:, target, :]]
        halo = jnp.where(live_slot[:, target, :, None], picked, jnp.zeros((), jnp.bfloat16))
        source = jnp.concatenate([neigh[target], halo.reshape(HALO_ROWS, HID)], axis=0)
        source = source.reshape(SRC_BLOCKS, TILE, HID).astype(jnp.float32)
        tiles_here = values[target].astype(jnp.float32)
        active = jnp.arange(TILES, dtype=jnp.int32) < live_tiles[target]
        products = jnp.einsum('tij,tjh->tih', tiles_here, source[tile_from[target]], precision=highest)
        placing = ((tile_into[target][None, :] == jnp.arange(LOCAL_BLOCKS, dtype=jnp.int32)[:, None]) & active[None, :]).astype(jnp.float32)
        summed = jnp.einsum('bt,tih->bih', placing, products, precision=highest).reshape(ROWS_DEV, HID)
        degree = 1.0 + jnp.dot(placing, lax.optimization_barrier(jnp.sum(tiles_here, axis=2)), precision=highest).reshape(ROWS_DEV)
        return (summed, degree)
    summed_all, degree_all = lax.map(aggregate, senders)
    degree = degree_all.reshape(NODES)
    pre = own + summed_all.reshape(NODES, HID) / degree[:, None]
    mean_pre = lax.optimization_barrier(jnp.sum(pre, axis=0)) / NODES
    variance = lax.optimization_barrier(jnp.sum(pre * pre, axis=0)) / NODES - mean_pre * mean_pre
    inverse = 1.0 / jnp.sqrt(variance + epsilon)
    normed = (pre - mean_pre) * inverse
    act = gain * normed + shift
    logistic = jax.nn.sigmoid(act)
    hidden = (act * logistic).astype(jnp.bfloat16)
    slope = d_hidden.reshape(NODES, HID).astype(jnp.float32) * logistic * (1.0 + act * (1.0 - logistic))
    shift_grad = lax.optimization_barrier(jnp.sum(slope, axis=0)) / NODES
    gain_grad = lax.optimization_barrier(jnp.sum(slope * normed, axis=0)) / NODES
    dpre = gain * inverse * (slope - shift_grad - normed * gain_grad)
    message_grad = (dpre / degree[:, None]).astype(jnp.bfloat16).reshape(PARTS_SIZE, LOCAL_BLOCKS, TILE, HID)

    def spread(running, target):
        tiles_here = values[target].astype(jnp.float32)
        active = jnp.arange(TILES, dtype=jnp.int32) < live_tiles[target]
        picked = message_grad[target][tile_into[target]].astype(jnp.float32)
        products = jnp.einsum('tij,tih->tjh', tiles_here, picked, precision=highest)
        placing = ((tile_from[target][None, :] == jnp.arange(SRC_BLOCKS, dtype=jnp.int32)[:, None]) & active[None, :]).astype(jnp.float32)
        source_grad = jnp.einsum('st,tjh->sjh', placing, products, precision=highest).reshape(SRC_BLOCKS * TILE, HID)
        running = running.at[target].add(source_grad[:ROWS_DEV])
        halo_grad = source_grad[ROWS_DEV:].astype(jnp.bfloat16)
        halo_grad = lax.optimization_barrier(halo_grad).astype(jnp.float32).reshape(PARTS_SIZE, SLOTS, HID)
        halo_grad = jnp.where(live_slot[:, target, :, None], halo_grad, jnp.zeros((), jnp.float32))
        running = running.at[senders[:, None], targets[:, target, :]].add(halo_grad)
        return (running, None)
    neigh_grad, _ = lax.scan(spread, jnp.zeros((PARTS_SIZE, ROWS_DEV, HID), jnp.float32), senders)
    out_shape = (FGROUPS, DGROUPS, ROWS_DEV, HID)
    return (hidden.reshape(out_shape), dpre.astype(jnp.bfloat16).reshape(out_shape), neigh_grad.astype(jnp.bfloat16).reshape(out_shape), gain_grad, shift_grad)
```

```python
import jax
import jax.numpy as jnp
from jax import lax
from jax.experimental import pallas as pl
from jax.experimental.pallas import tpu as pltpu
from jax.sharding import Mesh
from jax.sharding import PartitionSpec as P

FEAT_DOM = ("feat", "dom_0", "dom_1", "dom_2")
DOM = ("dom_0", "dom_1", "dom_2")
EPSILON = 1e-05
F32 = jnp.float32
BF16 = jnp.bfloat16
MIB = 1 << 20

VM = pl.BlockSpec(memory_space=pltpu.VMEM)
SM = pl.BlockSpec(memory_space=pltpu.SMEM)


def call(body, outs, ins, name, flops=0, moved=0, scratch=(), limit=24):
    return pl.pallas_call(
        body,
        out_shape=outs,
        in_specs=ins,
        out_specs=jax.tree.map(lambda _: VM, outs),
        scratch_shapes=list(scratch),
        name=name,
        compiler_params=pltpu.CompilerParams(vmem_limit_bytes=limit * MIB),
        cost_estimate=pl.CostEstimate(flops=flops, bytes_accessed=moved, transcendentals=0),
    )


def dot(a, b):
    return jnp.dot(a, b, preferred_element_type=F32)


def onehot_kernel(row_ref, col_ref, wide_ref, tall_ref):
    nodes, slots = wide_ref.shape
    step = 512

    def part(i, carry):
        at = pl.multiple_of(i * step, step)
        lane = row_ref[:, pl.ds(at, step)]
        down = lax.broadcasted_iota(jnp.int32, (nodes, step), 0)
        wide_ref[:, pl.ds(at, step)] = jnp.where(down == lane, 1.0, 0.0).astype(BF16)
        sub = col_ref[pl.ds(at, step), :]
        along = lax.broadcasted_iota(jnp.int32, (step, nodes), 1)
        tall_ref[pl.ds(at, step), :] = jnp.where(along == sub, 1.0, 0.0).astype(BF16)
        return carry

    lax.fori_loop(0, slots // step, part, 0)


def dense_kernel(src_ref, dst_ref, count_ref, vals_ref, al_ref, ah_ref, tl_ref, th_ref, rdeg_ref, acc_ref):
    size = vals_ref.shape[1]
    blocks = al_ref.shape[0] // size
    halo_blocks = ah_ref.shape[1] // size

    def clear(i, carry):
        for b in range(blocks):
            acc_ref[i * blocks + b] = jnp.zeros((size, size), F32)
        return carry

    lax.fori_loop(0, blocks + halo_blocks, clear, 0)

    def add(t, carry):
        at = src_ref[0, t] * blocks + dst_ref[0, t]
        acc_ref[at] += vals_ref[t].astype(F32)
        return carry

    lax.fori_loop(0, count_ref[0, 0], add, 0)

    for b in range(blocks):
        rdeg_ref[pl.ds(b * size, size), :] = jnp.zeros((size, size), F32)

    def place(wide_ref, tall_ref, first):
        def part(s, carry):
            at = pl.multiple_of(s * size, size)
            for b in range(blocks):
                tile = acc_ref[(s + first) * blocks + b]
                rdeg_ref[pl.ds(b * size, size), :] += tile
                wide_ref[pl.ds(b * size, size), pl.ds(at, size)] = tile.astype(BF16)
                tall_ref[pl.ds(at, size), pl.ds(b * size, size)] = tile.T.astype(BF16)
            return carry

        return part

    lax.fori_loop(0, blocks, place(al_ref, tl_ref, 0), 0)
    lax.fori_loop(0, halo_blocks, place(ah_ref, th_ref, blocks), 0)
    for b in range(blocks):
        rows = pl.ds(b * size, size)
        total = 1.0 + jnp.sum(rdeg_ref[rows, :], axis=1, keepdims=True)
        rdeg_ref[rows, :] = jnp.broadcast_to(1.0 / total, (size, size))


def gather_kernel(got_ref, tall_ref, neigh_ref, out_ref):
    groups = got_ref.shape[0]
    nodes = neigh_ref.shape[0]
    step = nodes
    total = dot(got_ref[0, :nodes, :], got_ref[0, nodes:, :])
    for g in range(1, groups):
        total += dot(got_ref[g, :nodes, :], got_ref[g, nodes:, :])
    neigh = total.astype(BF16)
    neigh_ref[...] = neigh

    def part(i, carry):
        at = pl.ds(pl.multiple_of(i * step, step), step)
        out_ref[at, :] = dot(tall_ref[at, :], neigh_ref[...]).astype(BF16)
        return carry

    lax.fori_loop(0, out_ref.shape[0] // step, part, 0)


def both_halves(rdeg):
    return jnp.concatenate([rdeg, rdeg], axis=1)


def base_kernel(got_ref, self_ref, al_ref, neigh_ref, rdeg_ref, base_ref):
    groups = got_ref.shape[0]
    nodes = neigh_ref.shape[0]
    cols = got_ref.shape[2]
    total = dot(got_ref[0, :nodes, :], self_ref[:cols, :])
    for g in range(1, groups):
        total += dot(got_ref[g, :nodes, :], self_ref[g * cols : (g + 1) * cols, :])
    near = dot(al_ref[...], neigh_ref[...])
    base_ref[...] = total + near * both_halves(rdeg_ref[...])


def put_sums(ref, first, second):
    half = ref.shape[1]
    ref[0:1, :] = first[:, :half]
    ref[1:2, :] = first[:, half:]
    ref[2:3, :] = second[:, :half]
    ref[3:4, :] = second[:, half:]


def get_sums(ref):
    first = jnp.concatenate([ref[0:1, :], ref[1:2, :]], axis=1)
    second = jnp.concatenate([ref[2:3, :], ref[3:4, :]], axis=1)
    return first, second


def pre_kernel(base_ref, ah_ref, halo_ref, rdeg_ref, pre_ref, sums_ref):
    step = 1024
    total = dot(ah_ref[:, :step], halo_ref[:step, :])
    for i in range(1, ah_ref.shape[1] // step):
        at = slice(i * step, (i + 1) * step)
        total += dot(ah_ref[:, at], halo_ref[at, :])
    pre = base_ref[...] + total * both_halves(rdeg_ref[...])
    pre_ref[...] = pre
    put_sums(sums_ref, jnp.sum(pre, axis=0, keepdims=True), jnp.sum(pre * pre, axis=0, keepdims=True))


def act_kernel(nodes_total, pre_ref, sums_ref, gain_ref, shift_ref, cot_ref, hidden_ref, slope_ref, normed_ref, scale_ref, out_ref):
    column, squares = get_sums(sums_ref)
    mean = column / nodes_total
    variance = squares / nodes_total - mean * mean
    inverse = 1.0 / jnp.sqrt(variance + EPSILON)
    normed = (pre_ref[...] - mean) * inverse
    act = gain_ref[...] * normed + shift_ref[...]
    logistic = 1.0 / (1.0 + jnp.exp(-act))
    hidden_ref[...] = (act * logistic).astype(BF16)
    slope = cot_ref[...].astype(F32) * logistic * (1.0 + act * (1.0 - logistic))
    slope_ref[...] = slope
    normed_ref[...] = normed
    scale_ref[...] = gain_ref[...] * inverse
    put_sums(out_ref, jnp.sum(slope, axis=0, keepdims=True), jnp.sum(slope * normed, axis=0, keepdims=True))


def back_kernel(nodes_total, slope_ref, normed_ref, sums_ref, scale_ref, rdeg_ref, th_ref, dself_ref, message_ref, grads_ref, out_ref):
    step = slope_ref.shape[0]
    first, second = get_sums(sums_ref)
    shift_grad = first / nodes_total
    gain_grad = second / nodes_total
    grads_ref[0:1, :] = gain_grad
    grads_ref[1:2, :] = shift_grad
    dpre = scale_ref[...] * (slope_ref[...] - shift_grad - normed_ref[...] * gain_grad)
    dself_ref[...] = dpre.astype(BF16)
    message_ref[...] = (dpre * both_halves(rdeg_ref[...])).astype(BF16)

    def part(i, carry):
        at = pl.ds(pl.multiple_of(i * step, step), step)
        out_ref[at, :] = dot(th_ref[at, :], message_ref[...]).astype(BF16)
        return carry

    lax.fori_loop(0, out_ref.shape[0] // step, part, 0)


def near_kernel(tl_ref, message_ref, out_ref):
    out_ref[...] = dot(tl_ref[...], message_ref[...])


def scatter_kernel(near_ref, wide_ref, back_ref, out_ref):
    step = 1024
    total = near_ref[...]
    for i in range(wide_ref.shape[1] // step):
        at = slice(i * step, (i + 1) * step)
        total += dot(wide_ref[:, at], back_ref[at, :])
    out_ref[...] = total.astype(BF16)


def exchange_sums(sums, devices):
    spread = jnp.broadcast_to(sums[None], (devices,) + sums.shape)
    return jnp.sum(lax.all_to_all(spread, FEAT_DOM, split_axis=0, concat_axis=0, tiled=True), axis=0)


def shards(
    features,
    w_self,
    w_neigh,
    gain,
    shift,
    d_hidden,
    send_rows,
    send_count,
    tile_src,
    tile_dst,
    tile_count,
    tile_vals,
):
    groups, _, nodes, cols = features.shape
    width = w_self.shape[1]
    tiles, size = tile_vals.shape[2:4]
    targets = send_rows[0, 0]
    parts_total, slot_count = targets.shape
    slots = parts_total * slot_count
    nodes_total = float(nodes * parts_total)
    shape = jax.ShapeDtypeStruct

    outbound = jnp.concatenate(
        [features.reshape(groups, nodes, cols), jnp.broadcast_to(w_neigh[None], (groups, cols, width))], axis=1
    )
    got = lax.all_to_all(outbound, "feat", split_axis=0, concat_axis=0, tiled=True)
    full_self = lax.all_gather(w_self, "feat", axis=0, tiled=True)

    live_slot = jnp.arange(slot_count)[None, :] < send_count[0, 0][:, None]
    chosen = jnp.where(live_slot, targets, -1)
    wide, tall = call(
        onehot_kernel,
        (shape((nodes, slots), BF16), shape((slots, nodes), BF16)),
        [VM, VM],
        "onehot",
        flops=8 * nodes * slots,
        moved=16 * MIB,
    )(chosen.reshape(1, slots), chosen.reshape(slots, 1))

    near_wide, far_wide, near_tall, far_tall, rdeg = call(
        dense_kernel,
        (
            shape((nodes, nodes), BF16),
            shape((nodes, slots), BF16),
            shape((nodes, nodes), BF16),
            shape((slots, nodes), BF16),
            shape((nodes, size), F32),
        ),
        [SM, SM, SM, VM],
        "dense",
        flops=16 * nodes * slots,
        moved=16 * MIB,
        scratch=[pltpu.VMEM(((nodes + slots) // size * (nodes // size), size, size), F32)],
        limit=32,
    )(tile_src[0], tile_dst[0], tile_count, tile_vals[0, 0])

    neigh, outgoing = call(
        gather_kernel,
        (shape((nodes, width), BF16), shape((slots, width), BF16)),
        [VM, VM],
        "gather",
        flops=2 * nodes * width * (slots + groups * cols),
        moved=8 * MIB,
    )(got, tall)

    halo = lax.all_to_all(
        outgoing.reshape(parts_total, slot_count, width), FEAT_DOM, split_axis=0, concat_axis=0, tiled=True
    ).reshape(slots, width)

    base = call(
        base_kernel,
        shape((nodes, width), F32),
        [VM] * 5,
        "base",
        flops=2 * nodes * width * (groups * cols + nodes),
        moved=4 * MIB,
    )(got, full_self, near_wide, neigh, rdeg)

    pre, sums = call(
        pre_kernel,
        (shape((nodes, width), F32), shape((4, width // 2), F32)),
        [VM] * 4,
        "pre",
        flops=2 * nodes * width * slots,
        moved=8 * MIB,
    )(base, far_wide, halo, rdeg)
    sums = exchange_sums(sums, parts_total)

    hidden, slope, normed, scale, grads = call(
        lambda *refs: act_kernel(nodes_total, *refs),
        (
            shape((nodes, width), BF16),
            shape((nodes, width), F32),
            shape((nodes, width), F32),
            shape((1, width), F32),
            shape((4, width // 2), F32),
        ),
        [VM] * 5,
        "act",
        flops=40 * nodes * width,
        moved=2 * MIB,
    )(pre, sums, gain.reshape(1, width), shift.reshape(1, width), d_hidden[0, 0])
    grads = exchange_sums(grads, parts_total)

    d_self, message, both_grads, leaving = call(
        lambda *refs: back_kernel(nodes_total, *refs),
        (
            shape((nodes, width), BF16),
            shape((nodes, width), BF16),
            shape((2, width), F32),
            shape((slots, width), BF16),
        ),
        [VM] * 6,
        "back",
        flops=2 * nodes * width * slots,
        moved=8 * MIB,
    )(slope, normed, grads, scale, rdeg, far_tall)

    returned = lax.all_to_all(
        leaving.reshape(parts_total, slot_count, width), FEAT_DOM, split_axis=0, concat_axis=0, tiled=True
    ).reshape(slots, width)
    near = call(
        near_kernel, shape((nodes, width), F32), [VM] * 2, "near", flops=2 * nodes * width * nodes, moved=2 * MIB
    )(near_tall, message)
    d_neigh = call(
        scatter_kernel,
        shape((nodes, width), BF16),
        [VM] * 3,
        "scatter",
        flops=2 * nodes * width * slots,
        moved=8 * MIB,
    )(near, wide, returned)

    out_shape = (1, 1, nodes, width)
    return (
        hidden.reshape(out_shape),
        d_self.reshape(out_shape),
        d_neigh.reshape(out_shape),
        both_grads[0],
        both_grads[1],
    )


def solution(mesh):
    split = Mesh(
        mesh.devices.reshape(mesh.shape["feat"], 4, 4, 2), ("feat", "dom_0", "dom_1", "dom_2")
    )
    placed = (
        P(None, DOM, None, "feat"),
        P("feat", None),
        P("feat", None),
        P(),
        P(),
        P("feat", DOM, None, None),
        P("feat", DOM, None, None),
        P("feat", DOM, None),
        P("feat", DOM, None),
        P("feat", DOM, None),
        P("feat", DOM),
        P("feat", DOM, None, None, None),
    )
    return jax.shard_map(
        shards,
        mesh=split,
        in_specs=placed,
        out_specs=(
            P("feat", DOM, None, None),
            P("feat", DOM, None, None),
            P("feat", DOM, None, None),
            P(),
            P(),
        ),
        check_vma=False,
    )
```

```python
import jax
import jax.numpy as jnp
from jax import lax
from jax.experimental import pallas as pl
from jax.experimental.pallas import tpu as pltpu
from jax.sharding import Mesh
from jax.sharding import PartitionSpec as P

FEAT_DOM = ("feat", "dom_0", "dom_1", "dom_2")
DOM = ("dom_0", "dom_1", "dom_2")
EPSILON = 1e-05
F32 = jnp.float32
BF16 = jnp.bfloat16
MIB = 1 << 20

VM = pl.BlockSpec(memory_space=pltpu.VMEM)
SM = pl.BlockSpec(memory_space=pltpu.SMEM)
ANY = pl.BlockSpec(memory_space=pl.ANY)
STEP = 512


def whole(*dims):
    return pl.BlockSpec(dims, lambda i: (0,) * len(dims))


def chunk(*dims):
    return pl.BlockSpec((None,) + dims, lambda i: (i,) + (0,) * len(dims))


def far(x):
    return pltpu.with_memory_space_constraint(x, pltpu.HBM)


def call(body, outs, ins, name, flops=0, moved=0, scratch=(), limit=40, out_specs=None, grid=()):
    return pl.pallas_call(
        body,
        grid=grid,
        out_shape=outs,
        in_specs=ins,
        out_specs=out_specs if out_specs is not None else jax.tree.map(lambda _: VM, outs),
        scratch_shapes=list(scratch),
        name=name,
        compiler_params=pltpu.CompilerParams(vmem_limit_bytes=limit * MIB),
        cost_estimate=pl.CostEstimate(flops=flops, bytes_accessed=moved, transcendentals=0),
    )


def dot(a, b):
    return jnp.dot(a, b, preferred_element_type=F32)


def tall_kernel(col_ref, tall_ref):
    along = lax.broadcasted_iota(jnp.int32, tall_ref.shape, 1)
    tall_ref[...] = jnp.where(along == col_ref[...], 1.0, 0.0).astype(BF16)


def wide_kernel(row_ref, wide_ref):
    down = lax.broadcasted_iota(jnp.int32, wide_ref.shape, 0)
    wide_ref[...] = jnp.where(down == row_ref[...], 1.0, 0.0).astype(BF16)


def dense_kernel(
    src_ref, dst_ref, count_ref, vals_hbm,
    al_ref, ah_hbm, tl_ref, th_hbm, rdeg_ref,
    acc_ref, vals_ref, wide_ref, tall_ref, in_sem, wide_sem, tall_sem,
):
    size = vals_ref.shape[1]
    blocks = al_ref.shape[0] // size
    chunks = wide_ref.shape[0]
    per_chunk = wide_ref.shape[2] // size
    parts = in_sem.shape[0]
    tiles = vals_ref.shape[0] // parts

    def arriving(c):
        at = pl.ds(c * tiles, tiles)
        return pltpu.make_async_copy(vals_hbm.at[at], vals_ref.at[at], in_sem.at[c])

    for c in range(parts):
        arriving(c).start()

    def clear(i, carry):
        for b in range(blocks):
            acc_ref[i * blocks + b] = jnp.zeros((size, size), F32)
        return carry

    lax.fori_loop(0, acc_ref.shape[0] // blocks, clear, 0)

    def add(t, carry):
        at = src_ref[0, t] * blocks + dst_ref[0, t]
        acc_ref[at] += vals_ref[t].astype(F32)
        return carry

    live = count_ref[0, 0]
    for c in range(parts):
        arriving(c).wait()
        lax.fori_loop(jnp.minimum(c * tiles, live), jnp.minimum((c + 1) * tiles, live), add, 0)

    rdeg_ref[...] = jnp.zeros(rdeg_ref.shape, F32)

    def place(s, put_wide, put_tall, at):
        for b in range(blocks):
            rows = slice(b * size, (b + 1) * size)
            tile = acc_ref[s * blocks + b]
            rdeg_ref[rows, :] += tile
            put_wide[rows, at * size : (at + 1) * size] = tile.astype(BF16)
            put_tall[at * size : (at + 1) * size, rows] = tile.T.astype(BF16)

    for s in range(blocks):
        place(s, al_ref, tl_ref, s)

    def leaving(c):
        return (
            pltpu.make_async_copy(wide_ref.at[c], ah_hbm.at[c], wide_sem.at[c]),
            pltpu.make_async_copy(tall_ref.at[c], th_hbm.at[c], tall_sem.at[c]),
        )

    def part(c, carry):
        for k in range(per_chunk):
            place(blocks + c * per_chunk + k, wide_ref.at[c], tall_ref.at[c], k)
        for copy in leaving(c):
            copy.start()
        return carry

    lax.fori_loop(0, chunks, part, 0)
    for b in range(blocks):
        rows = pl.ds(b * size, size)
        total = 1.0 + jnp.sum(rdeg_ref[rows, :], axis=1, keepdims=True)
        rdeg_ref[rows, :] = jnp.broadcast_to(1.0 / total, (size, size))
    for c in range(chunks):
        for copy in leaving(c):
            copy.wait()


def projected(me_ref, got_ref, weights):
    groups = got_ref.shape[0]
    me = me_ref[0]
    total = None
    for k, weight in enumerate(weights):
        term = dot(got_ref[lax.rem(me + k, groups)], weight[...])
        total = term if total is None else total + term
    return total


def gather_kernel(me_ref, got_ref, w0_ref, w1_ref, w2_ref, w3_ref, tall_ref, neigh_ref, out_ref):
    @pl.when(pl.program_id(0) == 0)
    def _():
        neigh_ref[...] = projected(me_ref, got_ref, (w0_ref, w1_ref, w2_ref, w3_ref)).astype(BF16)

    out_ref[...] = dot(tall_ref[...], neigh_ref[...]).astype(BF16)


def both_halves(rdeg):
    return jnp.concatenate([rdeg, rdeg], axis=1)


def base_kernel(me_ref, got_ref, w0_ref, w1_ref, w2_ref, w3_ref, al_ref, neigh_ref, rdeg_ref, base_ref):
    near = dot(al_ref[...], neigh_ref[...])
    own = projected(me_ref, got_ref, (w0_ref, w1_ref, w2_ref, w3_ref))
    base_ref[...] = own + near * both_halves(rdeg_ref[...])


def put_sums(ref, first, second):
    half = ref.shape[1]
    ref[0:1, :] = first[:, :half]
    ref[1:2, :] = first[:, half:]
    ref[2:3, :] = second[:, :half]
    ref[3:4, :] = second[:, half:]


def get_sums(ref):
    first = jnp.concatenate([ref[0:1, :], ref[1:2, :]], axis=1)
    second = jnp.concatenate([ref[2:3, :], ref[3:4, :]], axis=1)
    return first, second


def pre_kernel(base_ref, rdeg_ref, ah_ref, halo_ref, pre_ref, sums_ref):
    step = pl.program_id(0)
    term = dot(ah_ref[...], halo_ref[...])

    @pl.when(step == 0)
    def _():
        pre_ref[...] = term

    @pl.when(step > 0)
    def _():
        pre_ref[...] += term

    @pl.when(step == pl.num_programs(0) - 1)
    def _():
        pre = base_ref[...] + pre_ref[...] * both_halves(rdeg_ref[...])
        pre_ref[...] = pre
        put_sums(sums_ref, jnp.sum(pre, axis=0, keepdims=True), jnp.sum(pre * pre, axis=0, keepdims=True))


def act_kernel(nodes_total, pre_ref, sums_ref, gain_ref, shift_ref, cot_ref, hidden_ref, slope_ref, normed_ref, scale_ref, out_ref):
    column, squares = get_sums(sums_ref)
    mean = column / nodes_total
    variance = squares / nodes_total - mean * mean
    inverse = 1.0 / jnp.sqrt(variance + EPSILON)
    normed = (pre_ref[...] - mean) * inverse
    act = gain_ref[...] * normed + shift_ref[...]
    logistic = 1.0 / (1.0 + jnp.exp(-act))
    hidden_ref[...] = (act * logistic).astype(BF16)
    slope = cot_ref[...].astype(F32) * logistic * (1.0 + act * (1.0 - logistic))
    slope_ref[...] = slope
    normed_ref[...] = normed
    scale_ref[...] = gain_ref[...] * inverse
    put_sums(out_ref, jnp.sum(slope, axis=0, keepdims=True), jnp.sum(slope * normed, axis=0, keepdims=True))


def back_kernel(nodes_total, slope_ref, normed_ref, sums_ref, scale_ref, rdeg_ref, th_ref, dself_ref, message_ref, grads_ref, out_ref):
    @pl.when(pl.program_id(0) == 0)
    def _():
        first, second = get_sums(sums_ref)
        shift_grad = first / nodes_total
        gain_grad = second / nodes_total
        grads_ref[0:1, :] = gain_grad
        grads_ref[1:2, :] = shift_grad
        dpre = scale_ref[...] * (slope_ref[...] - shift_grad - normed_ref[...] * gain_grad)
        dself_ref[...] = dpre.astype(BF16)
        message_ref[...] = (dpre * both_halves(rdeg_ref[...])).astype(BF16)

    out_ref[...] = dot(th_ref[...], message_ref[...]).astype(BF16)


def near_kernel(tl_ref, message_ref, out_ref):
    out_ref[...] = dot(tl_ref[...], message_ref[...])


def scatter_kernel(near_ref, wide_ref, back_ref, out_ref, acc_ref):
    step = pl.program_id(0)
    term = dot(wide_ref[...], back_ref[...])

    @pl.when(step == 0)
    def _():
        acc_ref[...] = near_ref[...] + term

    @pl.when(step > 0)
    def _():
        acc_ref[...] += term

    @pl.when(step == pl.num_programs(0) - 1)
    def _():
        out_ref[...] = acc_ref[...].astype(BF16)


def exchange_sums(sums, devices):
    spread = jnp.broadcast_to(sums[None], (devices,) + sums.shape)
    return jnp.sum(lax.all_to_all(spread, FEAT_DOM, split_axis=0, concat_axis=0, tiled=True), axis=0)


def from_others(weight, groups):
    out = [weight]
    for k in range(1, groups):
        out.append(lax.ppermute(weight, "feat", [((j + k) % groups, j) for j in range(groups)]))
    return out


def shards(
    features,
    w_self,
    w_neigh,
    gain,
    shift,
    d_hidden,
    send_rows,
    send_count,
    tile_src,
    tile_dst,
    tile_count,
    tile_vals,
):
    groups, _, nodes, cols = features.shape
    width = w_self.shape[1]
    tiles, size = tile_vals.shape[2:4]
    targets = send_rows[0, 0]
    parts_total, slot_count = targets.shape
    slots = parts_total * slot_count
    chunks = slots // STEP
    nodes_total = float(nodes * parts_total)
    shape = jax.ShapeDtypeStruct
    hbm = pltpu.HBM
    me = lax.axis_index("feat").astype(jnp.int32).reshape(1)

    got = lax.all_to_all(features.reshape(groups, nodes, cols), "feat", split_axis=0, concat_axis=0, tiled=True)
    neigh_weights = from_others(w_neigh, groups)

    live_slot = jnp.arange(slot_count)[None, :] < send_count[0, 0][:, None]
    chosen = jnp.where(live_slot, targets, -1)
    tall = call(
        tall_kernel,
        hbm((chunks, STEP, nodes), BF16),
        [chunk(STEP, 1)],
        "tall",
        flops=4 * nodes * slots,
        moved=6 * MIB,
        out_specs=chunk(STEP, nodes),
        grid=(chunks,),
    )(chosen.reshape(chunks, STEP, 1))

    neigh, outgoing = call(
        gather_kernel,
        (hbm((nodes, width), BF16), hbm((chunks, STEP, width), BF16)),
        [SM, whole(groups, nodes, cols)] + [whole(cols, width)] * groups + [chunk(STEP, nodes)],
        "gather",
        flops=2 * nodes * width * (slots + groups * cols),
        moved=8 * MIB,
        out_specs=(whole(nodes, width), chunk(STEP, width)),
        grid=(chunks,),
    )(me, got, *neigh_weights, far(tall))

    halo = lax.all_to_all(
        outgoing.reshape(parts_total, slot_count, width), FEAT_DOM, split_axis=0, concat_axis=0, tiled=True
    ).reshape(chunks, STEP, width)

    late_chosen, late_src, neigh = lax.optimization_barrier((chosen, tile_src[0], neigh))
    wide = call(
        wide_kernel,
        hbm((chunks, nodes, STEP), BF16),
        [chunk(1, STEP)],
        "wide",
        flops=4 * nodes * slots,
        moved=4 * MIB,
        out_specs=chunk(nodes, STEP),
        grid=(chunks,),
    )(late_chosen.reshape(chunks, 1, STEP))

    near_wide, far_wide, near_tall, far_tall, rdeg = call(
        dense_kernel,
        (
            shape((nodes, nodes), BF16),
            hbm((chunks, nodes, STEP), BF16),
            shape((nodes, nodes), BF16),
            hbm((chunks, STEP, nodes), BF16),
            shape((nodes, size), F32),
        ),
        [SM, SM, SM, ANY],
        "dense",
        flops=16 * nodes * slots,
        moved=16 * MIB,
        scratch=[
            pltpu.VMEM(((nodes + slots) // size * (nodes // size), size, size), F32),
            pltpu.VMEM((tiles, size, size), BF16),
            pltpu.VMEM((chunks, nodes, STEP), BF16),
            pltpu.VMEM((chunks, STEP, nodes), BF16),
            pltpu.SemaphoreType.DMA((5,)),
            pltpu.SemaphoreType.DMA((chunks,)),
            pltpu.SemaphoreType.DMA((chunks,)),
        ],
        out_specs=(VM, ANY, VM, ANY, VM),
    )(late_src, tile_dst[0], tile_count, far(tile_vals[0, 0]))

    late_self, rdeg = lax.optimization_barrier((w_self, rdeg))
    self_weights = from_others(late_self, groups)
    base = call(
        base_kernel,
        hbm((nodes, width), F32),
        [SM] + [VM] * (groups + 4),
        "base",
        flops=2 * nodes * width * (groups * cols + nodes),
        moved=4 * MIB,
    )(me, got, *self_weights, near_wide, neigh, rdeg)

    pre, sums = call(
        pre_kernel,
        (shape((nodes, width), F32), shape((4, width // 2), F32)),
        [whole(nodes, width), whole(nodes, size), chunk(nodes, STEP), chunk(STEP, width)],
        "pre",
        flops=2 * nodes * width * slots,
        moved=8 * MIB,
        out_specs=(whole(nodes, width), whole(4, width // 2)),
        grid=(chunks,),
    )(far(base), rdeg, far(far_wide), halo)
    sums = exchange_sums(sums, parts_total)

    hidden, slope, normed, scale, grads = call(
        lambda *refs: act_kernel(nodes_total, *refs),
        (
            shape((nodes, width), BF16),
            shape((nodes, width), F32),
            shape((nodes, width), F32),
            shape((1, width), F32),
            shape((4, width // 2), F32),
        ),
        [VM] * 5,
        "act",
        flops=40 * nodes * width,
        moved=2 * MIB,
    )(pre, sums, gain.reshape(1, width), shift.reshape(1, width), d_hidden[0, 0])
    grads = exchange_sums(grads, parts_total)

    d_self, message, both_grads, leaving = call(
        lambda *refs: back_kernel(nodes_total, *refs),
        (
            shape((nodes, width), BF16),
            shape((nodes, width), BF16),
            shape((2, width), F32),
            hbm((chunks, STEP, width), BF16),
        ),
        [whole(nodes, width), whole(nodes, width), whole(4, width // 2), whole(1, width), whole(nodes, size), chunk(STEP, nodes)],
        "back",
        flops=2 * nodes * width * slots,
        moved=8 * MIB,
        out_specs=(whole(nodes, width), whole(nodes, width), whole(2, width), chunk(STEP, width)),
        grid=(chunks,),
    )(slope, normed, grads, scale, rdeg, far(far_tall))

    returned = lax.all_to_all(
        leaving.reshape(parts_total, slot_count, width), FEAT_DOM, split_axis=0, concat_axis=0, tiled=True
    ).reshape(chunks, STEP, width)
    near = call(
        near_kernel, shape((nodes, width), F32), [VM] * 2, "near", flops=2 * nodes * width * nodes, moved=2 * MIB
    )(near_tall, message)
    d_neigh = call(
        scatter_kernel,
        shape((nodes, width), BF16),
        [whole(nodes, width), chunk(nodes, STEP), chunk(STEP, width)],
        "scatter",
        flops=2 * nodes * width * slots,
        moved=8 * MIB,
        scratch=[pltpu.VMEM((nodes, width), F32)],
        out_specs=whole(nodes, width),
        grid=(chunks,),
    )(near, far(wide), returned)

    out_shape = (1, 1, nodes, width)
    return (
        hidden.reshape(out_shape),
        d_self.reshape(out_shape),
        d_neigh.reshape(out_shape),
        both_grads[0],
        both_grads[1],
    )


def solution(mesh):
    split = Mesh(
        mesh.devices.reshape(mesh.shape["feat"], 4, 4, 2), ("feat", "dom_0", "dom_1", "dom_2")
    )
    placed = (
        P(None, DOM, None, "feat"),
        P("feat", None),
        P("feat", None),
        P(),
        P(),
        P("feat", DOM, None, None),
        P("feat", DOM, None, None),
        P("feat", DOM, None),
        P("feat", DOM, None),
        P("feat", DOM, None),
        P("feat", DOM),
        P("feat", DOM, None, None, None),
    )
    return jax.shard_map(
        shards,
        mesh=split,
        in_specs=placed,
        out_specs=(
            P("feat", DOM, None, None),
            P("feat", DOM, None, None),
            P("feat", DOM, None, None),
            P(),
            P(),
        ),
        check_vma=False,
    )
```

```python
import jax
import jax.numpy as jnp
from jax import lax
from jax.experimental import pallas as pl
from jax.experimental.pallas import tpu as pltpu
from jax.sharding import Mesh
from jax.sharding import PartitionSpec as P

FEAT_DOM = ("feat", "dom_0", "dom_1", "dom_2")
DOM = ("dom_0", "dom_1", "dom_2")
EPSILON = 1e-05
F32 = jnp.float32
BF16 = jnp.bfloat16
MIB = 1 << 20

VM = pl.BlockSpec(memory_space=pltpu.VMEM)
SM = pl.BlockSpec(memory_space=pltpu.SMEM)
ANY = pl.BlockSpec(memory_space=pl.ANY)
STEP = 512
DEEP = 1024


def far(x):
    return pltpu.with_memory_space_constraint(x, pltpu.HBM)


def call(body, outs, ins, name, flops=0, moved=0, scratch=(), limit=40, out_specs=None):
    return pl.pallas_call(
        body,
        out_shape=outs,
        in_specs=ins,
        out_specs=out_specs if out_specs is not None else jax.tree.map(lambda _: VM, outs),
        scratch_shapes=list(scratch),
        name=name,
        compiler_params=pltpu.CompilerParams(vmem_limit_bytes=limit * MIB),
        cost_estimate=pl.CostEstimate(flops=flops, bytes_accessed=moved, transcendentals=0),
    )


def pieces(source, target, sems, each=1):
    count = source.shape[0] // each
    return [
        pltpu.make_async_copy(
            source.at[pl.ds(c * each, each)], target.at[pl.ds(c * each, each)], sems.at[c]
        )
        for c in range(count)
    ]


def dot(a, b):
    return jnp.dot(a, b, preferred_element_type=F32)


def tall_kernel(rows_ref, count_ref, tall_hbm, tall_ref, sems):
    slot_count, parts_total = rows_ref.shape
    chunks, step, nodes = tall_ref.shape
    per_chunk = step // slot_count
    order = lax.broadcasted_iota(jnp.int32, rows_ref.shape, 0)
    chosen = jnp.where(order < count_ref[...], rows_ref[...], -1)
    along = lax.broadcasted_iota(jnp.int32, (slot_count, nodes), 1)
    out = pieces(tall_ref, tall_hbm, sems)
    for q in range(parts_total):
        c, at = q // per_chunk, q % per_chunk * slot_count
        tall_ref[c, at : at + slot_count, :] = jnp.where(along == chosen[:, q : q + 1], 1.0, 0.0).astype(BF16)
        if q % per_chunk == per_chunk - 1:
            out[c].start()
    for copy in out:
        copy.wait()


def wide_kernel(row_ref, wide_hbm, wide_ref, sems):
    chunks, nodes, step = wide_ref.shape
    down = lax.broadcasted_iota(jnp.int32, (nodes, step), 0)
    out = pieces(wide_ref, wide_hbm, sems)
    for c in range(chunks):
        wide_ref[c] = jnp.where(down == row_ref[c], 1.0, 0.0).astype(BF16)
        out[c].start()
    for copy in out:
        copy.wait()


def dense_kernel(
    src_ref, dst_ref, count_ref, vals_hbm,
    al_ref, ah_hbm, tl_ref, th_hbm, rdeg_ref,
    acc_ref, vals_ref, wide_ref, tall_ref, in_sem, wide_sem, tall_sem,
):
    size = vals_ref.shape[1]
    blocks = al_ref.shape[0] // size
    chunks = wide_ref.shape[0]
    per_chunk = wide_ref.shape[2] // size
    parts = in_sem.shape[0]
    tiles = vals_ref.shape[0] // parts

    def arriving(c):
        at = pl.ds(c * tiles, tiles)
        return pltpu.make_async_copy(vals_hbm.at[at], vals_ref.at[at], in_sem.at[c])

    for c in range(parts):
        arriving(c).start()

    def clear(i, carry):
        for b in range(blocks):
            acc_ref[i * blocks + b] = jnp.zeros((size, size), F32)
        return carry

    lax.fori_loop(0, acc_ref.shape[0] // blocks, clear, 0)

    def add(t, carry):
        at = src_ref[0, t] * blocks + dst_ref[0, t]
        acc_ref[at] += vals_ref[t].astype(F32)
        return carry

    live = count_ref[0, 0]
    for c in range(parts):
        arriving(c).wait()
        lax.fori_loop(jnp.minimum(c * tiles, live), jnp.minimum((c + 1) * tiles, live), add, 0)

    rdeg_ref[...] = jnp.zeros(rdeg_ref.shape, F32)

    def place(s, put_wide, put_tall, at):
        for b in range(blocks):
            rows = slice(b * size, (b + 1) * size)
            tile = acc_ref[s * blocks + b]
            rdeg_ref[rows, :] += tile
            put_wide[rows, at * size : (at + 1) * size] = tile.astype(BF16)
            put_tall[at * size : (at + 1) * size, rows] = tile.T.astype(BF16)

    for s in range(blocks):
        place(s, al_ref, tl_ref, s)

    far_out = pieces(wide_ref, ah_hbm, wide_sem) + pieces(tall_ref, th_hbm, tall_sem)
    tall_per = tall_ref.shape[1] // size
    for s in range(chunks * per_chunk):
        place(
            blocks + s,
            wide_ref.at[s // per_chunk, :, pl.ds(s % per_chunk * size, size)],
            tall_ref.at[s // tall_per, pl.ds(s % tall_per * size, size), :],
            0,
        )
        if s % per_chunk == per_chunk - 1:
            far_out[s // per_chunk].start()
        if s % tall_per == tall_per - 1:
            far_out[chunks + s // tall_per].start()

    for b in range(blocks):
        rows = pl.ds(b * size, size)
        total = 1.0 + jnp.sum(rdeg_ref[rows, :], axis=1, keepdims=True)
        rdeg_ref[rows, :] = jnp.broadcast_to(1.0 / total, (size, size))
    for copy in far_out:
        copy.wait()


def projected(place_ref, got_ref, mine_ref, sent, weight_ref, which):
    groups, _, cols = got_ref.shape
    half = cols // 2
    me, core = place_ref[0], place_ref[1]
    total = dot(got_ref[me], mine_ref[...])
    rows = slice(which * half, (which + 1) * half)
    for k in range(1, groups):
        near_ref, far_ref = sent[2 * k - 2], sent[2 * k - 1]
        weight_ref[k - 1, pl.ds(pl.multiple_of(core * half, half), half), :] = near_ref[rows, :]
        weight_ref[k - 1, pl.ds(pl.multiple_of((1 - core) * half, half), half), :] = far_ref[rows, :]
        total += dot(got_ref[lax.rem(me + k, groups)], weight_ref[k - 1])
    return total


def gather_kernel(
    place_ref, got_ref, mine_ref, a1_ref, b1_ref, a2_ref, b2_ref, a3_ref, b3_ref, tall_hbm, neigh_hbm, out_hbm,
    tall_ref, neigh_ref, out_ref, weight_ref, in_sem, out_sem, neigh_sem,
):
    sent = (a1_ref, b1_ref, a2_ref, b2_ref, a3_ref, b3_ref)
    arriving = pieces(tall_hbm, tall_ref, in_sem)
    leaving = pieces(out_ref, out_hbm, out_sem)
    for copy in arriving:
        copy.start()
    neigh_ref[...] = projected(place_ref, got_ref, mine_ref, sent, weight_ref, 0).astype(BF16)
    keep = pltpu.make_async_copy(neigh_ref, neigh_hbm, neigh_sem)
    for c, (come, go) in enumerate(zip(arriving, leaving)):
        come.wait()
        out_ref[c] = dot(tall_ref[c], neigh_ref[...]).astype(BF16)
        go.start()
    keep.start()
    for copy in leaving:
        copy.wait()
    keep.wait()


def both_halves(rdeg):
    return jnp.concatenate([rdeg, rdeg], axis=1)


def base_kernel(
    place_ref, got_ref, mine_ref, a1_ref, b1_ref, a2_ref, b2_ref, a3_ref, b3_ref,
    al_ref, neigh_ref, rdeg_ref, base_ref, weight_ref,
):
    sent = (a1_ref, b1_ref, a2_ref, b2_ref, a3_ref, b3_ref)
    near = dot(al_ref[...], neigh_ref[...])
    own = projected(place_ref, got_ref, mine_ref, sent, weight_ref, 1)
    base_ref[...] = own + near * both_halves(rdeg_ref[...])


def put_sums(ref, first, second):
    half = ref.shape[1]
    ref[0:1, :] = first[:, :half]
    ref[1:2, :] = first[:, half:]
    ref[2:3, :] = second[:, :half]
    ref[3:4, :] = second[:, half:]


def get_sums(ref):
    first = jnp.concatenate([ref[0:1, :], ref[1:2, :]], axis=1)
    second = jnp.concatenate([ref[2:3, :], ref[3:4, :]], axis=1)
    return first, second


def pre_kernel(base_hbm, rdeg_ref, ah_hbm, halo_ref, pre_ref, sums_ref, ah_ref, base_ref, sems, base_sem):
    arriving = pieces(ah_hbm, ah_ref, sems)
    for copy in arriving:
        copy.start()
    late = pltpu.make_async_copy(base_hbm, base_ref, base_sem)
    late.start()
    for c, come in enumerate(arriving):
        come.wait()
        term = dot(ah_ref[c], halo_ref[c])
        if c == 0:
            pre_ref[...] = term
        elif c < len(arriving) - 1:
            pre_ref[...] += term
    late.wait()
    pre = base_ref[...] + (pre_ref[...] + term) * both_halves(rdeg_ref[...])
    pre_ref[...] = pre
    put_sums(sums_ref, jnp.sum(pre, axis=0, keepdims=True), jnp.sum(pre * pre, axis=0, keepdims=True))


def act_kernel(
    nodes_total, pre_ref, sums_ref, gain_ref, shift_ref, cot_hbm,
    hidden_hbm, slope_ref, normed_ref, scale_ref, out_ref, cot_ref, hidden_ref, sems,
):
    come = pltpu.make_async_copy(cot_hbm, cot_ref, sems.at[0])
    go = pltpu.make_async_copy(hidden_ref, hidden_hbm, sems.at[1])
    come.start()
    column, squares = get_sums(sums_ref)
    mean = column / nodes_total
    variance = squares / nodes_total - mean * mean
    inverse = 1.0 / jnp.sqrt(variance + EPSILON)
    scale_ref[...] = gain_ref[...] * inverse
    come.wait()
    normed = (pre_ref[...] - mean) * inverse
    act = gain_ref[...] * normed + shift_ref[...]
    logistic = 1.0 / (1.0 + jnp.exp(-act))
    hidden_ref[...] = (act * logistic).astype(BF16)
    slope = cot_ref[...].astype(F32) * logistic * (1.0 + act * (1.0 - logistic))
    slope_ref[...] = slope
    normed_ref[...] = normed
    go.start()
    put_sums(out_ref, jnp.sum(slope, axis=0, keepdims=True), jnp.sum(slope * normed, axis=0, keepdims=True))
    go.wait()


def back_kernel(
    nodes_total, slope_ref, normed_ref, sums_ref, scale_ref, rdeg_ref, th_hbm,
    dself_hbm, message_ref, grads_ref, out_hbm, th_ref, dself_ref, out_ref, in_sem, out_sem, dself_sem,
):
    arriving = pieces(th_hbm, th_ref, in_sem)
    leaving = pieces(out_ref, out_hbm, out_sem)
    keep = pltpu.make_async_copy(dself_ref, dself_hbm, dself_sem)
    for copy in arriving:
        copy.start()
    first, second = get_sums(sums_ref)
    shift_grad = first / nodes_total
    gain_grad = second / nodes_total
    grads_ref[0:1, :] = gain_grad
    grads_ref[1:2, :] = shift_grad
    dpre = scale_ref[...] * (slope_ref[...] - shift_grad - normed_ref[...] * gain_grad)
    dself_ref[...] = dpre.astype(BF16)
    message_ref[...] = (dpre * both_halves(rdeg_ref[...])).astype(BF16)
    for c, (come, go) in enumerate(zip(arriving, leaving)):
        come.wait()
        out_ref[c] = dot(th_ref[c], message_ref[...]).astype(BF16)
        go.start()
    keep.start()
    for copy in leaving:
        copy.wait()
    keep.wait()


def near_kernel(tl_ref, message_ref, out_ref):
    out_ref[...] = dot(tl_ref[...], message_ref[...])


def scatter_kernel(near_ref, wide_hbm, back_ref, out_ref, wide_ref, acc_ref, sems):
    arriving = pieces(wide_hbm, wide_ref, sems)
    for copy in arriving:
        copy.start()
    for c, come in enumerate(arriving):
        come.wait()
        term = dot(wide_ref[c], back_ref[c])
        if c == 0:
            acc_ref[...] = near_ref[...] + term
        elif c < len(arriving) - 1:
            acc_ref[...] += term
    out_ref[...] = (acc_ref[...] + term).astype(BF16)


def exchange_sums(sums, devices):
    spread = jnp.broadcast_to(sums[None], (devices,) + sums.shape)
    return jnp.sum(lax.all_to_all(spread, FEAT_DOM, split_axis=0, concat_axis=0, tiled=True), axis=0)


def from_others(w_neigh, w_self, groups):
    half = w_neigh.shape[0] // 2
    start = lax.axis_index("dom_2") * half
    mixed = jnp.concatenate([lax.dynamic_slice_in_dim(w, start, half, 0) for w in (w_neigh, w_self)], axis=0)
    out = []
    for k in range(1, groups):
        got = lax.ppermute(mixed, "feat", [((j + k) % groups, j) for j in range(groups)])
        out += [got, lax.ppermute(got, "dom_2", [(0, 1), (1, 0)])]
    return out


def shards(
    features,
    w_self,
    w_neigh,
    gain,
    shift,
    d_hidden,
    send_rows,
    send_count,
    tile_src,
    tile_dst,
    tile_count,
    tile_vals,
):
    groups, _, nodes, cols = features.shape
    width = w_self.shape[1]
    tiles, size = tile_vals.shape[2:4]
    targets = send_rows[0, 0]
    parts_total, slot_count = targets.shape
    slots = parts_total * slot_count
    chunks = slots // STEP
    nodes_total = float(nodes * parts_total)
    deep = slots // DEEP
    shape = jax.ShapeDtypeStruct
    hbm = pltpu.HBM
    buffer = pltpu.VMEM
    sems = pltpu.SemaphoreType.DMA
    place = jnp.stack([lax.axis_index("feat"), lax.axis_index("dom_2")]).astype(jnp.int32)

    got = lax.all_to_all(features.reshape(groups, nodes, cols), "feat", split_axis=0, concat_axis=0, tiled=True)
    sent = from_others(w_neigh, w_self, groups)

    tall = call(
        tall_kernel,
        hbm((chunks, STEP, nodes), BF16),
        [VM, VM],
        "tall",
        flops=4 * nodes * slots,
        moved=6 * MIB,
        scratch=[buffer((chunks, STEP, nodes), BF16), sems((chunks,))],
        out_specs=ANY,
    )(targets.T, send_count[0])

    neigh, outgoing = call(
        gather_kernel,
        (hbm((nodes, width), BF16), hbm((chunks, STEP, width), BF16)),
        [SM] + [VM] * (2 * groups) + [ANY],
        "gather",
        flops=2 * nodes * width * (slots + groups * cols),
        moved=8 * MIB,
        scratch=[
            buffer((chunks, STEP, nodes), BF16),
            buffer((nodes, width), BF16),
            buffer((chunks, STEP, width), BF16),
            buffer((groups - 1, cols, width), BF16),
            sems((chunks,)),
            sems((chunks,)),
            sems,
        ],
        out_specs=(ANY, ANY),
    )(place, got, w_neigh, *sent, far(tall))

    halo = lax.all_to_all(
        outgoing.reshape(parts_total, slot_count, width), FEAT_DOM, split_axis=0, concat_axis=0, tiled=True
    ).reshape(deep, DEEP, width)

    late_src, neigh = lax.optimization_barrier((tile_src[0], neigh))
    near_wide, far_wide, near_tall, far_tall, rdeg = call(
        dense_kernel,
        (
            shape((nodes, nodes), BF16),
            hbm((deep, nodes, DEEP), BF16),
            shape((nodes, nodes), BF16),
            hbm((chunks, STEP, nodes), BF16),
            shape((nodes, size), F32),
        ),
        [SM, SM, SM, ANY],
        "dense",
        flops=16 * nodes * slots,
        moved=16 * MIB,
        scratch=[
            buffer(((nodes + slots) // size * (nodes // size), size, size), F32),
            buffer((tiles, size, size), BF16),
            buffer((deep, nodes, DEEP), BF16),
            buffer((chunks, STEP, nodes), BF16),
            sems((5,)),
            sems((deep,)),
            sems((chunks,)),
        ],
        out_specs=(VM, ANY, VM, ANY, VM),
    )(late_src, tile_dst[0], tile_count, far(tile_vals[0, 0]))

    base = call(
        base_kernel,
        hbm((nodes, width), F32),
        [SM] + [VM] * (2 * groups + 3),
        "base",
        flops=2 * nodes * width * (groups * cols + nodes),
        moved=4 * MIB,
        scratch=[buffer((groups - 1, cols, width), BF16)],
    )(place, got, w_self, *sent, near_wide, neigh, rdeg)

    pre, sums = call(
        pre_kernel,
        (shape((nodes, width), F32), shape((4, width // 2), F32)),
        [ANY, VM, ANY, VM],
        "pre",
        flops=2 * nodes * width * slots,
        moved=8 * MIB,
        scratch=[buffer((deep, nodes, DEEP), BF16), buffer((nodes, width), F32), sems((deep,)), sems],
    )(far(base), rdeg, far(far_wide), halo)
    sums = exchange_sums(sums, parts_total)

    hidden, slope, normed, scale, grads = call(
        lambda *refs: act_kernel(nodes_total, *refs),
        (
            hbm((nodes, width), BF16),
            shape((nodes, width), F32),
            shape((nodes, width), F32),
            shape((1, width), F32),
            shape((4, width // 2), F32),
        ),
        [VM, VM, VM, VM, ANY],
        "act",
        flops=40 * nodes * width,
        moved=2 * MIB,
        scratch=[buffer((nodes, width), BF16), buffer((nodes, width), BF16), sems((2,))],
        out_specs=(ANY, VM, VM, VM, VM),
    )(pre, sums, gain.reshape(1, width), shift.reshape(1, width), far(d_hidden[0, 0]))
    grads = exchange_sums(grads, parts_total)

    d_self, message, both_grads, leaving = call(
        lambda *refs: back_kernel(nodes_total, *refs),
        (
            hbm((nodes, width), BF16),
            shape((nodes, width), BF16),
            shape((2, width), F32),
            hbm((chunks, STEP, width), BF16),
        ),
        [VM] * 5 + [ANY],
        "back",
        flops=2 * nodes * width * slots,
        moved=8 * MIB,
        scratch=[
            buffer((chunks, STEP, nodes), BF16),
            buffer((nodes, width), BF16),
            buffer((chunks, STEP, width), BF16),
            sems((chunks,)),
            sems((chunks,)),
            sems,
        ],
        out_specs=(ANY, VM, VM, ANY),
    )(slope, normed, grads, scale, rdeg, far(far_tall))

    returned = lax.all_to_all(
        leaving.reshape(parts_total, slot_count, width), FEAT_DOM, split_axis=0, concat_axis=0, tiled=True
    ).reshape(deep, DEEP, width)
    late_count, message = lax.optimization_barrier((send_count[0, 0], message))
    live_slot = jnp.arange(slot_count)[None, :] < late_count[:, None]
    wide = call(
        wide_kernel,
        hbm((deep, nodes, DEEP), BF16),
        [VM],
        "wide",
        flops=4 * nodes * slots,
        moved=4 * MIB,
        scratch=[buffer((deep, nodes, DEEP), BF16), sems((deep,))],
        out_specs=ANY,
    )(jnp.where(live_slot, targets, -1).reshape(deep, 1, DEEP))
    near = call(
        near_kernel, shape((nodes, width), F32), [VM] * 2, "near", flops=2 * nodes * width * nodes, moved=2 * MIB
    )(near_tall, message)
    d_neigh = call(
        scatter_kernel,
        shape((nodes, width), BF16),
        [VM, ANY, VM],
        "scatter",
        flops=2 * nodes * width * slots,
        moved=8 * MIB,
        scratch=[buffer((deep, nodes, DEEP), BF16), buffer((nodes, width), F32), sems((deep,))],
    )(near, far(wide), returned)

    out_shape = (1, 1, nodes, width)
    return (
        hidden.reshape(out_shape),
        d_self.reshape(out_shape),
        d_neigh.reshape(out_shape),
        both_grads[0],
        both_grads[1],
    )


def solution(mesh):
    split = Mesh(
        mesh.devices.reshape(mesh.shape["feat"], 4, 4, 2), ("feat", "dom_0", "dom_1", "dom_2")
    )
    placed = (
        P(None, DOM, None, "feat"),
        P("feat", None),
        P("feat", None),
        P(),
        P(),
        P("feat", DOM, None, None),
        P("feat", DOM, None, None),
        P("feat", DOM, None),
        P("feat", DOM, None),
        P("feat", DOM, None),
        P("feat", DOM),
        P("feat", DOM, None, None, None),
    )
    return jax.shard_map(
        shards,
        mesh=split,
        in_specs=placed,
        out_specs=(
            P("feat", DOM, None, None),
            P("feat", DOM, None, None),
            P("feat", DOM, None, None),
            P(),
            P(),
        ),
        check_vma=False,
    )
```

```python
import jax
import jax.numpy as jnp
from jax import lax
from jax.experimental import pallas as pl
from jax.experimental.pallas import tpu as pltpu
from jax.sharding import Mesh
from jax.sharding import PartitionSpec as P

FEAT_DOM = ("feat", "dom_0", "dom_1", "dom_2")
DOM = ("dom_0", "dom_1", "dom_2")
EPSILON = 1e-05
F32 = jnp.float32
BF16 = jnp.bfloat16
MIB = 1 << 20

VM = pl.BlockSpec(memory_space=pltpu.VMEM)
SM = pl.BlockSpec(memory_space=pltpu.SMEM)
ANY = pl.BlockSpec(memory_space=pl.ANY)
STEP = 512
DEEP = 1024


def far(x):
    return pltpu.with_memory_space_constraint(x, pltpu.HBM)


def call(body, outs, ins, name, flops=0, moved=0, scratch=(), limit=40, out_specs=None):
    return pl.pallas_call(
        body,
        out_shape=outs,
        in_specs=ins,
        out_specs=out_specs if out_specs is not None else jax.tree.map(lambda _: VM, outs),
        scratch_shapes=list(scratch),
        name=name,
        compiler_params=pltpu.CompilerParams(vmem_limit_bytes=limit * MIB),
        cost_estimate=pl.CostEstimate(flops=flops, bytes_accessed=moved, transcendentals=0),
    )


def pieces(source, target, sems, each=1):
    count = source.shape[0] // each
    return [
        pltpu.make_async_copy(
            source.at[pl.ds(c * each, each)], target.at[pl.ds(c * each, each)], sems.at[c]
        )
        for c in range(count)
    ]


def dot(a, b):
    return jnp.dot(a, b, preferred_element_type=F32)


def dense_kernel(
    src_ref, dst_ref, count_ref, vals_hbm,
    al_ref, ah_hbm, tl_ref, th_hbm, rdeg_ref,
    acc_ref, vals_ref, wide_ref, tall_ref, in_sem, wide_sem, tall_sem,
):
    size = vals_ref.shape[1]
    blocks = al_ref.shape[0] // size
    chunks = wide_ref.shape[0]
    per_chunk = wide_ref.shape[2] // size
    parts = in_sem.shape[0]
    tiles = vals_ref.shape[0] // parts

    def arriving(c):
        at = pl.ds(c * tiles, tiles)
        return pltpu.make_async_copy(vals_hbm.at[at], vals_ref.at[at], in_sem.at[c])

    for c in range(parts):
        arriving(c).start()

    def clear(i, carry):
        for b in range(blocks):
            acc_ref[i * blocks + b] = jnp.zeros((size, size), F32)
        return carry

    lax.fori_loop(0, acc_ref.shape[0] // blocks, clear, 0)

    def add(t, carry):
        at = src_ref[0, t] * blocks + dst_ref[0, t]
        acc_ref[at] += vals_ref[t].astype(F32)
        return carry

    live = count_ref[0, 0]
    for c in range(parts):
        arriving(c).wait()
        lax.fori_loop(jnp.minimum(c * tiles, live), jnp.minimum((c + 1) * tiles, live), add, 0)

    rdeg_ref[...] = jnp.zeros(rdeg_ref.shape, F32)

    def place(s, put_wide, put_tall, at):
        for b in range(blocks):
            rows = slice(b * size, (b + 1) * size)
            tile = acc_ref[s * blocks + b]
            rdeg_ref[rows, :] += tile
            put_wide[rows, at * size : (at + 1) * size] = tile.astype(BF16)
            put_tall[at * size : (at + 1) * size, rows] = tile.T.astype(BF16)

    for s in range(blocks):
        place(s, al_ref, tl_ref, s)

    far_out = pieces(wide_ref, ah_hbm, wide_sem) + pieces(tall_ref, th_hbm, tall_sem)
    tall_per = tall_ref.shape[1] // size
    for s in range(chunks * per_chunk):
        place(
            blocks + s,
            wide_ref.at[s // per_chunk, :, pl.ds(s % per_chunk * size, size)],
            tall_ref.at[s // tall_per, pl.ds(s % tall_per * size, size), :],
            0,
        )
        if s % per_chunk == per_chunk - 1:
            far_out[s // per_chunk].start()
        if s % tall_per == tall_per - 1:
            far_out[chunks + s // tall_per].start()

    for b in range(blocks):
        rows = pl.ds(b * size, size)
        total = 1.0 + jnp.sum(rdeg_ref[rows, :], axis=1, keepdims=True)
        rdeg_ref[rows, :] = jnp.broadcast_to(1.0 / total, (size, size))
    for copy in far_out:
        copy.wait()


def projected(me_ref, got_ref, weights):
    groups = got_ref.shape[0]
    me = me_ref[0]
    total = None
    for k, weight in enumerate(weights):
        term = dot(got_ref[lax.rem(me + k, groups)], weight[...])
        total = term if total is None else total + term
    return total


def gather_kernel(
    me_ref, got_ref, w0_ref, w1_ref, w2_ref, w3_ref, rows_ref, count_ref, neigh_hbm, out_hbm,
    tall_ref, neigh_ref, out_ref, out_sem, neigh_sem,
):
    slot_count = rows_ref.shape[0]
    chunks, step, nodes = tall_ref.shape
    per_chunk = step // slot_count
    leaving = pieces(out_ref, out_hbm, out_sem)
    order = lax.broadcasted_iota(jnp.int32, rows_ref.shape, 0)
    chosen = jnp.where(order < count_ref[...], rows_ref[...], -1)
    along = lax.broadcasted_iota(jnp.int32, (slot_count, nodes), 1)
    neigh_ref[...] = projected(me_ref, got_ref, (w0_ref, w1_ref, w2_ref, w3_ref)).astype(BF16)
    keep = pltpu.make_async_copy(neigh_ref, neigh_hbm, neigh_sem)
    keep.start()
    for c, go in enumerate(leaving):
        for k in range(per_chunk):
            q = c * per_chunk + k
            hot = jnp.where(along == chosen[:, q : q + 1], 1.0, 0.0).astype(BF16)
            tall_ref[c, k * slot_count : (k + 1) * slot_count, :] = hot
        out_ref[c] = dot(tall_ref[c], neigh_ref[...]).astype(BF16)
        go.start()
    for copy in leaving:
        copy.wait()
    keep.wait()


def both_halves(rdeg):
    return jnp.concatenate([rdeg, rdeg], axis=1)


def base_kernel(
    me_ref, got_ref, w0_ref, w1_hbm, w2_hbm, w3_hbm, al_ref, neigh_ref, rdeg_ref, base_ref, w1_ref, w2_ref, w3_ref, sems,
):
    pairs = ((w1_hbm, w1_ref), (w2_hbm, w2_ref), (w3_hbm, w3_ref))
    copies = [pltpu.make_async_copy(a, b, sems.at[i]) for i, (a, b) in enumerate(pairs)]
    for copy in copies:
        copy.start()
    near = dot(al_ref[...], neigh_ref[...])
    for copy in copies:
        copy.wait()
    own = projected(me_ref, got_ref, (w0_ref, w1_ref, w2_ref, w3_ref))
    base_ref[...] = own + near * both_halves(rdeg_ref[...])


def put_sums(ref, first, second):
    half = ref.shape[1]
    ref[0:1, :] = first[:, :half]
    ref[1:2, :] = first[:, half:]
    ref[2:3, :] = second[:, :half]
    ref[3:4, :] = second[:, half:]


def get_sums(ref):
    first = jnp.concatenate([ref[0:1, :], ref[1:2, :]], axis=1)
    second = jnp.concatenate([ref[2:3, :], ref[3:4, :]], axis=1)
    return first, second


def pre_kernel(base_hbm, rdeg_ref, ah_hbm, halo_ref, pre_ref, sums_ref, ah_ref, base_ref, sems, base_sem):
    arriving = pieces(ah_hbm, ah_ref, sems)
    for copy in arriving:
        copy.start()
    late = pltpu.make_async_copy(base_hbm, base_ref, base_sem)
    late.start()
    for c, come in enumerate(arriving):
        come.wait()
        term = dot(ah_ref[c], halo_ref[c])
        if c == 0:
            pre_ref[...] = term
        elif c < len(arriving) - 1:
            pre_ref[...] += term
    late.wait()
    pre = base_ref[...] + (pre_ref[...] + term) * both_halves(rdeg_ref[...])
    pre_ref[...] = pre
    put_sums(sums_ref, jnp.sum(pre, axis=0, keepdims=True), jnp.sum(pre * pre, axis=0, keepdims=True))


def act_kernel(
    nodes_total, pre_ref, sums_ref, gain_ref, shift_ref, cot_hbm,
    hidden_hbm, slope_ref, normed_ref, scale_ref, out_ref, cot_ref, hidden_ref, sems,
):
    come = pltpu.make_async_copy(cot_hbm, cot_ref, sems.at[0])
    go = pltpu.make_async_copy(hidden_ref, hidden_hbm, sems.at[1])
    come.start()
    column, squares = get_sums(sums_ref)
    mean = column / nodes_total
    variance = squares / nodes_total - mean * mean
    inverse = 1.0 / jnp.sqrt(variance + EPSILON)
    scale_ref[...] = gain_ref[...] * inverse
    come.wait()
    normed = (pre_ref[...] - mean) * inverse
    act = gain_ref[...] * normed + shift_ref[...]
    logistic = 1.0 / (1.0 + jnp.exp(-act))
    hidden_ref[...] = (act * logistic).astype(BF16)
    slope = cot_ref[...].astype(F32) * logistic * (1.0 + act * (1.0 - logistic))
    slope_ref[...] = slope
    normed_ref[...] = normed
    go.start()
    put_sums(out_ref, jnp.sum(slope, axis=0, keepdims=True), jnp.sum(slope * normed, axis=0, keepdims=True))
    go.wait()


def back_kernel(
    nodes_total, slope_ref, normed_ref, sums_ref, scale_ref, rdeg_ref, th_hbm,
    dself_hbm, message_hbm, grads_ref, out_hbm, th_ref, dself_ref, message_ref, out_ref, in_sem, out_sem, keep_sem,
):
    arriving = pieces(th_hbm, th_ref, in_sem)
    leaving = pieces(out_ref, out_hbm, out_sem)
    keeping = [
        pltpu.make_async_copy(dself_ref, dself_hbm, keep_sem.at[0]),
        pltpu.make_async_copy(message_ref, message_hbm, keep_sem.at[1]),
    ]
    for copy in arriving[:2]:
        copy.start()
    first, second = get_sums(sums_ref)
    shift_grad = first / nodes_total
    gain_grad = second / nodes_total
    grads_ref[0:1, :] = gain_grad
    grads_ref[1:2, :] = shift_grad
    dpre = scale_ref[...] * (slope_ref[...] - shift_grad - normed_ref[...] * gain_grad)
    dself_ref[...] = dpre.astype(BF16)
    message_ref[...] = (dpre * both_halves(rdeg_ref[...])).astype(BF16)
    for c, (come, go) in enumerate(zip(arriving, leaving)):
        come.wait()
        if c + 2 < len(arriving):
            arriving[c + 2].start()
        out_ref[c] = dot(th_ref[c], message_ref[...]).astype(BF16)
        go.start()
    for copy in keeping:
        copy.start()
    for copy in leaving + keeping:
        copy.wait()


def near_kernel(tl_ref, message_ref, out_ref):
    out_ref[...] = dot(tl_ref[...], message_ref[...])


def scatter_kernel(near_ref, row_ref, back_ref, out_ref, acc_ref):
    deep, step, _ = back_ref.shape
    nodes = out_ref.shape[0]
    down = lax.broadcasted_iota(jnp.int32, (nodes, step), 0)
    acc_ref[...] = near_ref[...]
    for c in range(deep):
        wide = jnp.where(down == row_ref[c], 1.0, 0.0).astype(BF16)
        acc_ref[...] += dot(wide, back_ref[c])
    out_ref[...] = acc_ref[...].astype(BF16)


def exchange_sums(sums, devices):
    spread = jnp.broadcast_to(sums[None], (devices,) + sums.shape)
    return jnp.sum(lax.all_to_all(spread, FEAT_DOM, split_axis=0, concat_axis=0, tiled=True), axis=0)


def from_others(weight, groups):
    out = [weight]
    for k in range(1, groups):
        out.append(lax.ppermute(weight, "feat", [((j + k) % groups, j) for j in range(groups)]))
    return out


def shards(
    features,
    w_self,
    w_neigh,
    gain,
    shift,
    d_hidden,
    send_rows,
    send_count,
    tile_src,
    tile_dst,
    tile_count,
    tile_vals,
):
    groups, _, nodes, cols = features.shape
    width = w_self.shape[1]
    tiles, size = tile_vals.shape[2:4]
    targets = send_rows[0, 0]
    parts_total, slot_count = targets.shape
    slots = parts_total * slot_count
    chunks = slots // STEP
    nodes_total = float(nodes * parts_total)
    deep = slots // DEEP
    shape = jax.ShapeDtypeStruct
    hbm = pltpu.HBM
    buffer = pltpu.VMEM
    sems = pltpu.SemaphoreType.DMA
    me = lax.axis_index("feat").astype(jnp.int32).reshape(1)

    got = lax.all_to_all(features.reshape(groups, nodes, cols), "feat", split_axis=0, concat_axis=0, tiled=True)
    neigh_weights = from_others(w_neigh, groups)

    neigh, outgoing = call(
        gather_kernel,
        (hbm((nodes, width), BF16), hbm((chunks, STEP, width), BF16)),
        [SM] + [VM] * (groups + 3),
        "gather",
        flops=2 * nodes * width * (slots + groups * cols),
        moved=8 * MIB,
        scratch=[
            buffer((chunks, STEP, nodes), BF16),
            buffer((nodes, width), BF16),
            buffer((chunks, STEP, width), BF16),
            sems((chunks,)),
            sems,
        ],
        out_specs=(ANY, ANY),
    )(me, got, *neigh_weights, targets.T, send_count[0])
    outgoing, *self_weights = lax.optimization_barrier((outgoing, *from_others(w_self, groups)))

    halo = lax.all_to_all(
        outgoing.reshape(parts_total, slot_count, width), FEAT_DOM, split_axis=0, concat_axis=0, tiled=True
    ).reshape(deep, DEEP, width)

    late_src, neigh = lax.optimization_barrier((tile_src[0], neigh))
    near_wide, far_wide, near_tall, far_tall, rdeg = call(
        dense_kernel,
        (
            shape((nodes, nodes), BF16),
            hbm((deep, nodes, DEEP), BF16),
            shape((nodes, nodes), BF16),
            hbm((deep, DEEP, nodes), BF16),
            shape((nodes, size), F32),
        ),
        [SM, SM, SM, ANY],
        "dense",
        flops=16 * nodes * slots,
        moved=16 * MIB,
        scratch=[
            buffer(((nodes + slots) // size * (nodes // size), size, size), F32),
            buffer((tiles, size, size), BF16),
            buffer((deep, nodes, DEEP), BF16),
            buffer((deep, DEEP, nodes), BF16),
            sems((5,)),
            sems((deep,)),
            sems((deep,)),
        ],
        out_specs=(VM, ANY, VM, ANY, VM),
    )(late_src, tile_dst[0], tile_count, far(tile_vals[0, 0]))

    base = call(
        base_kernel,
        hbm((nodes, width), F32),
        [SM, VM, VM, ANY, ANY, ANY, VM, VM, VM],
        "base",
        flops=2 * nodes * width * (groups * cols + nodes),
        moved=4 * MIB,
        scratch=[buffer((cols, width), BF16)] * 3 + [sems((3,))],
    )(me, got, self_weights[0], *map(far, self_weights[1:]), near_wide, neigh, rdeg)

    pre, sums = call(
        pre_kernel,
        (shape((nodes, width), F32), shape((4, width // 2), F32)),
        [ANY, VM, ANY, VM],
        "pre",
        flops=2 * nodes * width * slots,
        moved=8 * MIB,
        scratch=[buffer((deep, nodes, DEEP), BF16), buffer((nodes, width), F32), sems((deep,)), sems],
    )(far(base), rdeg, far(far_wide), halo)
    sums = exchange_sums(sums, parts_total)

    hidden, slope, normed, scale, grads = call(
        lambda *refs: act_kernel(nodes_total, *refs),
        (
            hbm((nodes, width), BF16),
            shape((nodes, width), F32),
            shape((nodes, width), F32),
            shape((1, width), F32),
            shape((4, width // 2), F32),
        ),
        [VM, VM, VM, VM, ANY],
        "act",
        flops=40 * nodes * width,
        moved=2 * MIB,
        scratch=[buffer((nodes, width), BF16), buffer((nodes, width), BF16), sems((2,))],
        out_specs=(ANY, VM, VM, VM, VM),
    )(pre, sums, gain.reshape(1, width), shift.reshape(1, width), far(d_hidden[0, 0]))
    grads = exchange_sums(grads, parts_total)

    d_self, message, both_grads, leaving = call(
        lambda *refs: back_kernel(nodes_total, *refs),
        (
            hbm((nodes, width), BF16),
            hbm((nodes, width), BF16),
            shape((2, width), F32),
            hbm((deep, DEEP, width), BF16),
        ),
        [VM] * 5 + [ANY],
        "back",
        flops=2 * nodes * width * slots,
        moved=8 * MIB,
        scratch=[
            buffer((deep, DEEP, nodes), BF16),
            buffer((nodes, width), BF16),
            buffer((nodes, width), BF16),
            buffer((deep, DEEP, width), BF16),
            sems((deep,)),
            sems((deep,)),
            sems((2,)),
        ],
        out_specs=(ANY, ANY, VM, ANY),
    )(slope, normed, grads, scale, rdeg, far(far_tall))

    returned = lax.all_to_all(
        leaving.reshape(parts_total, slot_count, width), FEAT_DOM, split_axis=0, concat_axis=0, tiled=True
    ).reshape(deep, DEEP, width)
    late_count, message = lax.optimization_barrier((send_count[0, 0], message))
    live_slot = jnp.arange(slot_count)[None, :] < late_count[:, None]
    chosen = jnp.where(live_slot, targets, -1).reshape(deep, 1, DEEP)
    near = call(
        near_kernel, shape((nodes, width), F32), [VM] * 2, "near", flops=2 * nodes * width * nodes, moved=2 * MIB
    )(near_tall, message)
    d_neigh = call(
        scatter_kernel,
        shape((nodes, width), BF16),
        [VM] * 3,
        "scatter",
        flops=2 * nodes * width * slots,
        moved=8 * MIB,
        scratch=[buffer((nodes, width), F32)],
    )(near, chosen, returned)

    out_shape = (1, 1, nodes, width)
    return (
        hidden.reshape(out_shape),
        d_self.reshape(out_shape),
        d_neigh.reshape(out_shape),
        both_grads[0],
        both_grads[1],
    )


def solution(mesh):
    split = Mesh(
        mesh.devices.reshape(mesh.shape["feat"], 4, 4, 2), ("feat", "dom_0", "dom_1", "dom_2")
    )
    placed = (
        P(None, DOM, None, "feat"),
        P("feat", None),
        P("feat", None),
        P(),
        P(),
        P("feat", DOM, None, None),
        P("feat", DOM, None, None),
        P("feat", DOM, None),
        P("feat", DOM, None),
        P("feat", DOM, None),
        P("feat", DOM),
        P("feat", DOM, None, None, None),
    )
    return jax.shard_map(
        shards,
        mesh=split,
        in_specs=placed,
        out_specs=(
            P("feat", DOM, None, None),
            P("feat", DOM, None, None),
            P("feat", DOM, None, None),
            P(),
            P(),
        ),
        check_vma=False,
    )
```

```python
import jax
import jax.numpy as jnp
from jax import lax
from jax.experimental import pallas as pl
from jax.experimental.pallas import tpu as pltpu
from jax.sharding import Mesh
from jax.sharding import PartitionSpec as P

FEAT_DOM = ("feat", "dom_0", "dom_1", "dom_2")
DOM = ("dom_0", "dom_1", "dom_2")
EPSILON = 1e-05
F32 = jnp.float32
BF16 = jnp.bfloat16
MIB = 1 << 20

VM = pl.BlockSpec(memory_space=pltpu.VMEM)
SM = pl.BlockSpec(memory_space=pltpu.SMEM)
ANY = pl.BlockSpec(memory_space=pl.ANY)
STEP = 512
DEEP = 1024


def far(x):
    return pltpu.with_memory_space_constraint(x, pltpu.HBM)


def call(body, outs, ins, name, flops=0, moved=0, scratch=(), limit=40, out_specs=None):
    return pl.pallas_call(
        body,
        out_shape=outs,
        in_specs=ins,
        out_specs=out_specs if out_specs is not None else jax.tree.map(lambda _: VM, outs),
        scratch_shapes=list(scratch),
        name=name,
        compiler_params=pltpu.CompilerParams(vmem_limit_bytes=limit * MIB),
        cost_estimate=pl.CostEstimate(flops=flops, bytes_accessed=moved, transcendentals=0),
    )


def pieces(source, target, sems, each=1):
    count = source.shape[0] // each
    return [
        pltpu.make_async_copy(
            source.at[pl.ds(c * each, each)], target.at[pl.ds(c * each, each)], sems.at[c]
        )
        for c in range(count)
    ]


def dot(a, b):
    return jnp.dot(a, b, preferred_element_type=F32)


def dense_kernel(
    src_ref, dst_ref, count_ref, vals_hbm,
    al_ref, ah_hbm, tl_ref, th_hbm, rdeg_ref,
    acc_ref, vals_ref, wide_ref, tall_ref, in_sem, wide_sem, tall_sem,
):
    size = vals_ref.shape[1]
    blocks = al_ref.shape[0] // size
    chunks = wide_ref.shape[0]
    per_chunk = wide_ref.shape[2] // size
    parts = in_sem.shape[0]
    tiles = vals_ref.shape[0] // parts

    def arriving(c):
        at = pl.ds(c * tiles, tiles)
        return pltpu.make_async_copy(vals_hbm.at[at], vals_ref.at[at], in_sem.at[c])

    for c in range(parts):
        arriving(c).start()

    def clear(i, carry):
        for b in range(blocks):
            acc_ref[i * blocks + b] = jnp.zeros((size, size), F32)
        return carry

    lax.fori_loop(0, acc_ref.shape[0] // blocks, clear, 0)

    def add(t, carry):
        at = src_ref[0, t] * blocks + dst_ref[0, t]
        acc_ref[at] += vals_ref[t].astype(F32)
        return carry

    live = count_ref[0, 0]
    for c in range(parts):
        arriving(c).wait()
        lax.fori_loop(jnp.minimum(c * tiles, live), jnp.minimum((c + 1) * tiles, live), add, 0)

    rdeg_ref[...] = jnp.zeros(rdeg_ref.shape, F32)

    def place(s, put_wide, put_tall, at):
        for b in range(blocks):
            rows = slice(b * size, (b + 1) * size)
            tile = acc_ref[s * blocks + b]
            rdeg_ref[rows, :] += tile
            put_wide[rows, at * size : (at + 1) * size] = tile.astype(BF16)
            put_tall[at * size : (at + 1) * size, rows] = tile.T.astype(BF16)

    for s in range(blocks):
        place(s, al_ref, tl_ref, s)

    far_out = pieces(wide_ref, ah_hbm, wide_sem) + pieces(tall_ref, th_hbm, tall_sem)
    tall_per = tall_ref.shape[1] // size
    for s in range(chunks * per_chunk):
        place(
            blocks + s,
            wide_ref.at[s // per_chunk, :, pl.ds(s % per_chunk * size, size)],
            tall_ref.at[s // tall_per, pl.ds(s % tall_per * size, size), :],
            0,
        )
        if s % per_chunk == per_chunk - 1:
            far_out[s // per_chunk].start()
        if s % tall_per == tall_per - 1:
            far_out[chunks + s // tall_per].start()

    for b in range(blocks):
        rows = pl.ds(b * size, size)
        total = 1.0 + jnp.sum(rdeg_ref[rows, :], axis=1, keepdims=True)
        rdeg_ref[rows, :] = jnp.broadcast_to(1.0 / total, (size, size))
    for copy in far_out:
        copy.wait()


def projected(got_ref, weights):
    groups = got_ref.shape[0]
    me = lax.axis_index("feat")
    total = None
    for k, weight in enumerate(weights):
        term = dot(got_ref[lax.rem(me + k, groups)], weight[...])
        total = term if total is None else total + term
    return total


def gather_kernel(
    got_ref, w0_ref, w1_ref, w2_ref, w3_ref, rows_ref, count_ref, neigh_hbm, out_hbm,
    tall_ref, neigh_ref, out_ref, out_sem, neigh_sem,
):
    slot_count = rows_ref.shape[0]
    chunks, step, nodes = tall_ref.shape
    per_chunk = step // slot_count
    leaving = pieces(out_ref, out_hbm, out_sem)
    order = lax.broadcasted_iota(jnp.int32, rows_ref.shape, 0)
    chosen = jnp.where(order < count_ref[...], rows_ref[...], -1)
    along = lax.broadcasted_iota(jnp.int32, (slot_count, nodes), 1)
    neigh_ref[...] = projected(got_ref, (w0_ref, w1_ref, w2_ref, w3_ref)).astype(BF16)
    keep = pltpu.make_async_copy(neigh_ref, neigh_hbm, neigh_sem)
    keep.start()
    for c, go in enumerate(leaving):
        for k in range(per_chunk):
            q = c * per_chunk + k
            hot = jnp.where(along == chosen[:, q : q + 1], 1.0, 0.0).astype(BF16)
            tall_ref[c, k * slot_count : (k + 1) * slot_count, :] = hot
        out_ref[c] = dot(tall_ref[c], neigh_ref[...]).astype(BF16)
        go.start()
    for copy in leaving:
        copy.wait()
    keep.wait()


def both_halves(rdeg):
    return jnp.concatenate([rdeg, rdeg], axis=1)


def base_kernel(
    got_ref, w0_ref, a1_ref, a2_ref, a3_ref, b1_ref, b2_ref, b3_ref, al_ref, neigh_ref, rdeg_ref, base_ref, weight_ref
):
    half = a1_ref.shape[0]
    core = lax.axis_index("dom_2")
    mine = pl.ds(pl.multiple_of(core * half, half), half)
    other = pl.ds(pl.multiple_of((1 - core) * half, half), half)
    for k, (a, b) in enumerate(((a1_ref, b1_ref), (a2_ref, b2_ref), (a3_ref, b3_ref))):
        weight_ref[k, mine, :] = a[...]
        weight_ref[k, other, :] = b[...]
    near = dot(al_ref[...], neigh_ref[...])
    own = projected(got_ref, (w0_ref, weight_ref.at[0], weight_ref.at[1], weight_ref.at[2]))
    base_ref[...] = own + near * both_halves(rdeg_ref[...])


def put_sums(ref, first, second):
    half = ref.shape[1]
    ref[0:1, :] = first[:, :half]
    ref[1:2, :] = first[:, half:]
    ref[2:3, :] = second[:, :half]
    ref[3:4, :] = second[:, half:]


def get_sums(ref):
    first = jnp.concatenate([ref[0:1, :], ref[1:2, :]], axis=1)
    second = jnp.concatenate([ref[2:3, :], ref[3:4, :]], axis=1)
    return first, second


def pre_kernel(base_hbm, rdeg_ref, ah_hbm, halo_ref, pre_ref, sums_ref, ah_ref, base_ref, sems, base_sem):
    arriving = pieces(ah_hbm, ah_ref, sems)
    for copy in arriving:
        copy.start()
    late = pltpu.make_async_copy(base_hbm, base_ref, base_sem)
    late.start()
    for c, come in enumerate(arriving):
        come.wait()
        term = dot(ah_ref[c], halo_ref[c])
        if c == 0:
            pre_ref[...] = term
        elif c < len(arriving) - 1:
            pre_ref[...] += term
    late.wait()
    pre = base_ref[...] + (pre_ref[...] + term) * both_halves(rdeg_ref[...])
    pre_ref[...] = pre
    put_sums(sums_ref, jnp.sum(pre, axis=0, keepdims=True), jnp.sum(pre * pre, axis=0, keepdims=True))


def act_kernel(
    nodes_total, pre_ref, sums_ref, gain_ref, shift_ref, cot_hbm,
    hidden_hbm, slope_ref, normed_ref, scale_ref, out_ref, cot_ref, hidden_ref, sems,
):
    come = pltpu.make_async_copy(cot_hbm, cot_ref, sems.at[0])
    go = pltpu.make_async_copy(hidden_ref, hidden_hbm, sems.at[1])
    come.start()
    column, squares = get_sums(sums_ref)
    mean = column / nodes_total
    variance = squares / nodes_total - mean * mean
    inverse = 1.0 / jnp.sqrt(variance + EPSILON)
    scale_ref[...] = gain_ref[...] * inverse
    normed = (pre_ref[...] - mean) * inverse
    act = gain_ref[...] * normed + shift_ref[...]
    logistic = 1.0 / (1.0 + jnp.exp(-act))
    hidden_ref[...] = (act * logistic).astype(BF16)
    normed_ref[...] = normed
    slope_ref[...] = logistic * (1.0 + act * (1.0 - logistic))
    go.start()
    come.wait()
    slope = cot_ref[...].astype(F32) * slope_ref[...]
    slope_ref[...] = slope
    put_sums(
        out_ref, jnp.sum(slope, axis=0, keepdims=True), jnp.sum(slope * normed_ref[...], axis=0, keepdims=True)
    )
    go.wait()


def back_kernel(
    nodes_total, slope_ref, normed_ref, sums_ref, scale_ref, rdeg_ref, th_hbm,
    dself_hbm, message_hbm, grads_ref, out_hbm, th_ref, dself_ref, message_ref, out_ref, in_sem, out_sem, keep_sem,
):
    arriving = pieces(th_hbm, th_ref, in_sem)
    leaving = pieces(out_ref, out_hbm, out_sem)
    keeping = [
        pltpu.make_async_copy(dself_ref, dself_hbm, keep_sem.at[0]),
        pltpu.make_async_copy(message_ref, message_hbm, keep_sem.at[1]),
    ]
    half = len(arriving) // 2
    for copy in arriving[:half]:
        copy.start()
    first, second = get_sums(sums_ref)
    shift_grad = first / nodes_total
    gain_grad = second / nodes_total
    grads_ref[0:1, :] = gain_grad
    grads_ref[1:2, :] = shift_grad
    dpre = scale_ref[...] * (slope_ref[...] - shift_grad - normed_ref[...] * gain_grad)
    dself_ref[...] = dpre.astype(BF16)
    message_ref[...] = (dpre * both_halves(rdeg_ref[...])).astype(BF16)
    for copy in arriving[half:]:
        copy.start()
    for c, go in enumerate(leaving):
        if c % half == 0:
            for come in arriving[c : c + half]:
                come.wait()
        out_ref[c] = dot(th_ref[c], message_ref[...]).astype(BF16)
        go.start()
    for copy in keeping:
        copy.start()
    for copy in leaving + keeping:
        copy.wait()


def near_kernel(tl_ref, message_ref, out_ref):
    out_ref[...] = dot(tl_ref[...], message_ref[...])


def scatter_kernel(near_ref, row_ref, back_ref, out_ref, acc_ref):
    deep, step, _ = back_ref.shape
    nodes = out_ref.shape[0]
    down = lax.broadcasted_iota(jnp.int32, (nodes, step), 0)
    acc_ref[...] = near_ref[...]
    for c in range(deep):
        wide = jnp.where(down == row_ref[c], 1.0, 0.0).astype(BF16)
        acc_ref[...] += dot(wide, back_ref[c])
    out_ref[...] = acc_ref[...].astype(BF16)


def exchange_sums(sums, devices):
    spread = jnp.broadcast_to(sums[None], (devices,) + sums.shape)
    return jnp.sum(lax.all_to_all(spread, FEAT_DOM, split_axis=0, concat_axis=0, tiled=True), axis=0)


def from_others(weight, groups):
    out = [weight]
    for k in range(1, groups):
        out.append(lax.ppermute(weight, "feat", [((j + k) % groups, j) for j in range(groups)]))
    return out


def shards(
    features,
    w_self,
    w_neigh,
    gain,
    shift,
    d_hidden,
    send_rows,
    send_count,
    tile_src,
    tile_dst,
    tile_count,
    tile_vals,
):
    groups, _, nodes, cols = features.shape
    width = w_self.shape[1]
    tiles, size = tile_vals.shape[2:4]
    targets = send_rows[0, 0]
    parts_total, slot_count = targets.shape
    slots = parts_total * slot_count
    chunks = slots // STEP
    nodes_total = float(nodes * parts_total)
    deep = slots // DEEP
    shape = jax.ShapeDtypeStruct
    hbm = pltpu.HBM
    buffer = pltpu.VMEM
    sems = pltpu.SemaphoreType.DMA

    got = lax.all_to_all(features.reshape(groups, nodes, cols), "feat", split_axis=0, concat_axis=0, tiled=True)
    neigh_weights = from_others(w_neigh, groups)

    neigh, outgoing = call(
        gather_kernel,
        (hbm((nodes, width), BF16), hbm((chunks, STEP, width), BF16)),
        [VM] * (groups + 3),
        "gather",
        flops=2 * nodes * width * (slots + groups * cols),
        moved=8 * MIB,
        scratch=[
            buffer((chunks, STEP, nodes), BF16),
            buffer((nodes, width), BF16),
            buffer((chunks, STEP, width), BF16),
            sems((chunks,)),
            sems,
        ],
        out_specs=(ANY, ANY),
    )(got, *neigh_weights, targets.T, send_count[0])
    half = cols // 2
    mine = lax.dynamic_slice_in_dim(w_self, lax.axis_index("dom_2") * half, half, 0)
    outgoing, *self_mine = lax.optimization_barrier((outgoing, *from_others(mine, groups)[1:]))
    self_other = [lax.ppermute(w, "dom_2", [(0, 1), (1, 0)]) for w in self_mine]

    halo = lax.all_to_all(
        outgoing.reshape(parts_total, slot_count, width), FEAT_DOM, split_axis=0, concat_axis=0, tiled=True
    ).reshape(deep, DEEP, width)

    late_src, neigh = lax.optimization_barrier((tile_src[0], neigh))
    near_wide, far_wide, near_tall, far_tall, rdeg = call(
        dense_kernel,
        (
            shape((nodes, nodes), BF16),
            hbm((deep, nodes, DEEP), BF16),
            shape((nodes, nodes), BF16),
            hbm((deep, DEEP, nodes), BF16),
            shape((nodes, size), F32),
        ),
        [SM, SM, SM, ANY],
        "dense",
        flops=16 * nodes * slots,
        moved=16 * MIB,
        scratch=[
            buffer(((nodes + slots) // size * (nodes // size), size, size), F32),
            buffer((tiles, size, size), BF16),
            buffer((deep, nodes, DEEP), BF16),
            buffer((deep, DEEP, nodes), BF16),
            sems((5,)),
            sems((deep,)),
            sems((deep,)),
        ],
        out_specs=(VM, ANY, VM, ANY, VM),
    )(late_src, tile_dst[0], tile_count, far(tile_vals[0, 0]))

    base = call(
        base_kernel,
        hbm((nodes, width), F32),
        [VM] * (2 * groups + 3),
        "base",
        flops=2 * nodes * width * (groups * cols + nodes),
        moved=4 * MIB,
        scratch=[buffer((groups - 1, cols, width), BF16)],
    )(got, w_self, *self_mine, *self_other, near_wide, neigh, rdeg)

    pre, sums = call(
        pre_kernel,
        (shape((nodes, width), F32), shape((4, width // 2), F32)),
        [ANY, VM, ANY, VM],
        "pre",
        flops=2 * nodes * width * slots,
        moved=8 * MIB,
        scratch=[buffer((deep, nodes, DEEP), BF16), buffer((nodes, width), F32), sems((deep,)), sems],
    )(far(base), rdeg, far(far_wide), halo)
    sums = exchange_sums(sums, parts_total)

    hidden, slope, normed, scale, grads = call(
        lambda *refs: act_kernel(nodes_total, *refs),
        (
            hbm((nodes, width), BF16),
            shape((nodes, width), F32),
            shape((nodes, width), F32),
            shape((1, width), F32),
            shape((4, width // 2), F32),
        ),
        [VM, VM, VM, VM, ANY],
        "act",
        flops=40 * nodes * width,
        moved=2 * MIB,
        scratch=[buffer((nodes, width), BF16), buffer((nodes, width), BF16), sems((2,))],
        out_specs=(ANY, VM, VM, VM, VM),
    )(pre, sums, gain.reshape(1, width), shift.reshape(1, width), far(d_hidden[0, 0]))
    grads = exchange_sums(grads, parts_total)

    d_self, message, both_grads, leaving = call(
        lambda *refs: back_kernel(nodes_total, *refs),
        (
            hbm((nodes, width), BF16),
            hbm((nodes, width), BF16),
            shape((2, width), F32),
            hbm((deep, DEEP, width), BF16),
        ),
        [VM] * 5 + [ANY],
        "back",
        flops=2 * nodes * width * slots,
        moved=8 * MIB,
        scratch=[
            buffer((deep, DEEP, nodes), BF16),
            buffer((nodes, width), BF16),
            buffer((nodes, width), BF16),
            buffer((deep, DEEP, width), BF16),
            sems((deep,)),
            sems((deep,)),
            sems((2,)),
        ],
        out_specs=(ANY, ANY, VM, ANY),
    )(slope, normed, grads, scale, rdeg, far(far_tall))

    returned = lax.all_to_all(
        leaving.reshape(parts_total, slot_count, width), FEAT_DOM, split_axis=0, concat_axis=0, tiled=True
    ).reshape(deep, DEEP, width)
    late_count, message = lax.optimization_barrier((send_count[0, 0], message))
    live_slot = jnp.arange(slot_count)[None, :] < late_count[:, None]
    chosen = jnp.where(live_slot, targets, -1).reshape(deep, 1, DEEP)
    near = call(
        near_kernel, shape((nodes, width), F32), [VM] * 2, "near", flops=2 * nodes * width * nodes, moved=2 * MIB
    )(near_tall, message)
    d_neigh = call(
        scatter_kernel,
        shape((nodes, width), BF16),
        [VM] * 3,
        "scatter",
        flops=2 * nodes * width * slots,
        moved=8 * MIB,
        scratch=[buffer((nodes, width), F32)],
    )(near, chosen, returned)

    out_shape = (1, 1, nodes, width)
    return (
        hidden.reshape(out_shape),
        d_self.reshape(out_shape),
        d_neigh.reshape(out_shape),
        both_grads[0],
        both_grads[1],
    )


def solution(mesh):
    split = Mesh(
        mesh.devices.reshape(mesh.shape["feat"], 4, 4, 2), ("feat", "dom_0", "dom_1", "dom_2")
    )
    placed = (
        P(None, DOM, None, "feat"),
        P("feat", None),
        P("feat", None),
        P(),
        P(),
        P("feat", DOM, None, None),
        P("feat", DOM, None, None),
        P("feat", DOM, None),
        P("feat", DOM, None),
        P("feat", DOM, None),
        P("feat", DOM),
        P("feat", DOM, None, None, None),
    )
    return jax.shard_map(
        shards,
        mesh=split,
        in_specs=placed,
        out_specs=(
            P("feat", DOM, None, None),
            P("feat", DOM, None, None),
            P("feat", DOM, None, None),
            P(),
            P(),
        ),
        check_vma=False,
    )
```

```python
import jax
import jax.numpy as jnp
from jax import lax
from jax.experimental import pallas as pl
from jax.experimental.pallas import tpu as pltpu
from jax.sharding import Mesh
from jax.sharding import PartitionSpec as P

FEAT_DOM = ("feat", "dom_0", "dom_1", "dom_2")
DOM = ("dom_0", "dom_1", "dom_2")
EPSILON = 1e-05
F32 = jnp.float32
BF16 = jnp.bfloat16
MIB = 1 << 20

VM = pl.BlockSpec(memory_space=pltpu.VMEM)
SM = pl.BlockSpec(memory_space=pltpu.SMEM)
ANY = pl.BlockSpec(memory_space=pl.ANY)
STEP = 512
DEEP = 1024


def far(x):
    return pltpu.with_memory_space_constraint(x, pltpu.HBM)


def call(body, outs, ins, name, flops=0, moved=0, scratch=(), limit=40, out_specs=None):
    return pl.pallas_call(
        body,
        out_shape=outs,
        in_specs=ins,
        out_specs=out_specs if out_specs is not None else jax.tree.map(lambda _: VM, outs),
        scratch_shapes=list(scratch),
        name=name,
        compiler_params=pltpu.CompilerParams(vmem_limit_bytes=limit * MIB),
        cost_estimate=pl.CostEstimate(flops=flops, bytes_accessed=moved, transcendentals=0),
    )


def pieces(source, target, sems, each=1):
    count = source.shape[0] // each
    return [
        pltpu.make_async_copy(
            source.at[pl.ds(c * each, each)], target.at[pl.ds(c * each, each)], sems.at[c]
        )
        for c in range(count)
    ]


def dot(a, b):
    return jnp.dot(a, b, preferred_element_type=F32)


def dense_kernel(
    src_ref, dst_ref, count_ref, vals_hbm,
    al_ref, ah_hbm, tl_ref, th_hbm, rdeg_ref,
    acc_ref, vals_ref, wide_ref, tall_ref, in_sem, wide_sem, tall_sem,
):
    size = vals_ref.shape[1]
    blocks = al_ref.shape[0] // size
    chunks = wide_ref.shape[0]
    per_chunk = wide_ref.shape[2] // size
    parts = in_sem.shape[0]
    tiles = vals_ref.shape[0] // parts

    def arriving(c):
        at = pl.ds(c * tiles, tiles)
        return pltpu.make_async_copy(vals_hbm.at[at], vals_ref.at[at], in_sem.at[c])

    for c in range(parts):
        arriving(c).start()

    def clear(i, carry):
        for b in range(blocks):
            acc_ref[i * blocks + b] = jnp.zeros((size, size), F32)
        return carry

    lax.fori_loop(0, acc_ref.shape[0] // blocks, clear, 0)

    def add(t, carry):
        at = src_ref[0, t] * blocks + dst_ref[0, t]
        acc_ref[at] += vals_ref[t].astype(F32)
        return carry

    live = count_ref[0, 0]
    for c in range(parts):
        arriving(c).wait()
        lax.fori_loop(jnp.minimum(c * tiles, live), jnp.minimum((c + 1) * tiles, live), add, 0)

    rdeg_ref[...] = jnp.zeros(rdeg_ref.shape, F32)

    def place(s, put_wide, put_tall, at):
        for b in range(blocks):
            rows = slice(b * size, (b + 1) * size)
            tile = acc_ref[s * blocks + b]
            rdeg_ref[rows, :] += tile
            put_wide[rows, at * size : (at + 1) * size] = tile.astype(BF16)
            put_tall[at * size : (at + 1) * size, rows] = tile.T.astype(BF16)

    for s in range(blocks):
        place(s, al_ref, tl_ref, s)

    far_out = pieces(wide_ref, ah_hbm, wide_sem) + pieces(tall_ref, th_hbm, tall_sem)
    tall_per = tall_ref.shape[1] // size
    for s in range(chunks * per_chunk):
        place(
            blocks + s,
            wide_ref.at[s // per_chunk, :, pl.ds(s % per_chunk * size, size)],
            tall_ref.at[s // tall_per, pl.ds(s % tall_per * size, size), :],
            0,
        )
        if s % per_chunk == per_chunk - 1:
            far_out[s // per_chunk].start()
        if s % tall_per == tall_per - 1:
            far_out[chunks + s // tall_per].start()

    for b in range(blocks):
        rows = pl.ds(b * size, size)
        total = 1.0 + jnp.sum(rdeg_ref[rows, :], axis=1, keepdims=True)
        rdeg_ref[rows, :] = jnp.broadcast_to(1.0 / total, (size, size))
    for copy in far_out:
        copy.wait()


def projected(blocks, mine_ref, sent, weight_ref, which):
    half = mine_ref.shape[0] // 2
    core = lax.axis_index("dom_2")
    near = pl.ds(pl.multiple_of(core * half, half), half)
    far = pl.ds(pl.multiple_of((1 - core) * half, half), half)
    rows = slice(which * half, (which + 1) * half)
    total = dot(blocks[0][...], mine_ref[...])
    for k, (a, b) in enumerate(sent):
        weight_ref[k, near, :] = a[rows, :]
        weight_ref[k, far, :] = b[rows, :]
        total += dot(blocks[k + 1][...], weight_ref[k])
    return total


def gather_kernel(
    f0_ref, f2_ref, f3_ref, f1_ref, neigh_w_ref, self_w_ref, a2_ref, b2_ref, a3_ref, b3_ref, a1_ref, b1_ref,
    rows_ref, count_ref, neigh_hbm, own_ref, out_hbm, tall_ref, neigh_ref, out_ref, weight_ref, out_sem, neigh_sem,
):
    blocks = (f0_ref, f1_ref, f2_ref, f3_ref)
    sent = ((a1_ref, b1_ref), (a2_ref, b2_ref), (a3_ref, b3_ref))
    slot_count = rows_ref.shape[0]
    chunks, step, nodes = tall_ref.shape
    per_chunk = step // slot_count
    leaving = pieces(out_ref, out_hbm, out_sem)
    order = lax.broadcasted_iota(jnp.int32, rows_ref.shape, 0)
    chosen = jnp.where(order < count_ref[...], rows_ref[...], -1)
    along = lax.broadcasted_iota(jnp.int32, (slot_count, nodes), 1)
    neigh_ref[...] = projected(blocks, neigh_w_ref, sent, weight_ref.at[0], 0).astype(BF16)
    keep = pltpu.make_async_copy(neigh_ref, neigh_hbm, neigh_sem)
    keep.start()
    for c, go in enumerate(leaving):
        for k in range(per_chunk):
            q = c * per_chunk + k
            hot = jnp.where(along == chosen[:, q : q + 1], 1.0, 0.0).astype(BF16)
            tall_ref[c, k * slot_count : (k + 1) * slot_count, :] = hot
        out_ref[c] = dot(tall_ref[c], neigh_ref[...]).astype(BF16)
        go.start()
    own_ref[...] = projected(blocks, self_w_ref, sent, weight_ref.at[1], 1)
    for copy in leaving:
        copy.wait()
    keep.wait()


def both_halves(rdeg):
    return jnp.concatenate([rdeg, rdeg], axis=1)


def base_kernel(own_ref, al_ref, neigh_ref, rdeg_ref, base_ref):
    base_ref[...] = own_ref[...] + dot(al_ref[...], neigh_ref[...]) * both_halves(rdeg_ref[...])


def put_sums(ref, first, second):
    half = ref.shape[1]
    ref[0:1, :] = first[:, :half]
    ref[1:2, :] = first[:, half:]
    ref[2:3, :] = second[:, :half]
    ref[3:4, :] = second[:, half:]


def get_sums(ref):
    first = jnp.concatenate([ref[0:1, :], ref[1:2, :]], axis=1)
    second = jnp.concatenate([ref[2:3, :], ref[3:4, :]], axis=1)
    return first, second


def pre_kernel(base_hbm, rdeg_ref, ah_hbm, halo_ref, pre_ref, sums_ref, ah_ref, base_ref, sems, base_sem):
    arriving = pieces(ah_hbm, ah_ref, sems)
    for copy in arriving:
        copy.start()
    late = pltpu.make_async_copy(base_hbm, base_ref, base_sem)
    late.start()
    for c, come in enumerate(arriving):
        come.wait()
        term = dot(ah_ref[c], halo_ref[c])
        if c == 0:
            pre_ref[...] = term
        elif c < len(arriving) - 1:
            pre_ref[...] += term
    late.wait()
    pre = base_ref[...] + (pre_ref[...] + term) * both_halves(rdeg_ref[...])
    pre_ref[...] = pre
    put_sums(sums_ref, jnp.sum(pre, axis=0, keepdims=True), jnp.sum(pre * pre, axis=0, keepdims=True))


def act_kernel(
    nodes_total, pre_ref, sums_ref, gain_ref, shift_ref, cot_hbm,
    hidden_hbm, slope_ref, normed_ref, scale_ref, out_ref, cot_ref, hidden_ref, sems,
):
    come = pltpu.make_async_copy(cot_hbm, cot_ref, sems.at[0])
    go = pltpu.make_async_copy(hidden_ref, hidden_hbm, sems.at[1])
    come.start()
    column, squares = get_sums(sums_ref)
    mean = column / nodes_total
    variance = squares / nodes_total - mean * mean
    inverse = 1.0 / jnp.sqrt(variance + EPSILON)
    scale_ref[...] = gain_ref[...] * inverse
    normed = (pre_ref[...] - mean) * inverse
    act = gain_ref[...] * normed + shift_ref[...]
    logistic = 1.0 / (1.0 + jnp.exp(-act))
    hidden_ref[...] = (act * logistic).astype(BF16)
    normed_ref[...] = normed
    slope_ref[...] = logistic * (1.0 + act * (1.0 - logistic))
    go.start()
    come.wait()
    slope = cot_ref[...].astype(F32) * slope_ref[...]
    slope_ref[...] = slope
    put_sums(
        out_ref, jnp.sum(slope, axis=0, keepdims=True), jnp.sum(slope * normed_ref[...], axis=0, keepdims=True)
    )
    go.wait()


def back_kernel(
    nodes_total, slope_ref, normed_ref, sums_ref, scale_ref, rdeg_ref, th_hbm,
    dself_hbm, message_hbm, grads_ref, out_hbm, th_ref, dself_ref, message_ref, out_ref, in_sem, out_sem, keep_sem,
):
    arriving = pieces(th_hbm, th_ref, in_sem)
    leaving = pieces(out_ref, out_hbm, out_sem)
    keeping = [
        pltpu.make_async_copy(dself_ref, dself_hbm, keep_sem.at[0]),
        pltpu.make_async_copy(message_ref, message_hbm, keep_sem.at[1]),
    ]
    half = len(arriving) // 2
    for copy in arriving[:half]:
        copy.start()
    first, second = get_sums(sums_ref)
    shift_grad = first / nodes_total
    gain_grad = second / nodes_total
    grads_ref[0:1, :] = gain_grad
    grads_ref[1:2, :] = shift_grad
    dpre = scale_ref[...] * (slope_ref[...] - shift_grad - normed_ref[...] * gain_grad)
    dself_ref[...] = dpre.astype(BF16)
    message_ref[...] = (dpre * both_halves(rdeg_ref[...])).astype(BF16)
    for copy in arriving[half:]:
        copy.start()
    for c, go in enumerate(leaving):
        if c % half == 0:
            for come in arriving[c : c + half]:
                come.wait()
        out_ref[c] = dot(th_ref[c], message_ref[...]).astype(BF16)
        go.start()
    for copy in keeping:
        copy.start()
    for copy in leaving + keeping:
        copy.wait()


def near_kernel(tl_ref, message_ref, out_ref):
    out_ref[...] = dot(tl_ref[...], message_ref[...])


def scatter_kernel(near_ref, row_ref, back_ref, out_ref, acc_ref):
    deep, step, _ = back_ref.shape
    nodes = out_ref.shape[0]
    down = lax.broadcasted_iota(jnp.int32, (nodes, step), 0)
    acc_ref[...] = near_ref[...]
    for c in range(deep):
        wide = jnp.where(down == row_ref[c], 1.0, 0.0).astype(BF16)
        acc_ref[...] += dot(wide, back_ref[c])
    out_ref[...] = acc_ref[...].astype(BF16)


def exchange_sums(sums, devices):
    spread = jnp.broadcast_to(sums[None], (devices,) + sums.shape)
    return jnp.sum(lax.all_to_all(spread, FEAT_DOM, split_axis=0, concat_axis=0, tiled=True), axis=0)


def shifted(array, k, groups):
    return lax.ppermute(array, "feat", [((j + k) % groups, j) for j in range(groups)])


def shards(
    features,
    w_self,
    w_neigh,
    gain,
    shift,
    d_hidden,
    send_rows,
    send_count,
    tile_src,
    tile_dst,
    tile_count,
    tile_vals,
):
    groups, _, nodes, cols = features.shape
    width = w_self.shape[1]
    tiles, size = tile_vals.shape[2:4]
    targets = send_rows[0, 0]
    parts_total, slot_count = targets.shape
    slots = parts_total * slot_count
    chunks = slots // STEP
    nodes_total = float(nodes * parts_total)
    deep = slots // DEEP
    shape = jax.ShapeDtypeStruct
    hbm = pltpu.HBM
    buffer = pltpu.VMEM
    sems = pltpu.SemaphoreType.DMA

    core_half = cols // 2
    start = lax.axis_index("dom_2") * core_half
    mixed = jnp.concatenate(
        [lax.dynamic_slice_in_dim(w, start, core_half, 0) for w in (w_neigh, w_self)], axis=0
    )
    feature_blocks, mixed = lax.optimization_barrier((features.reshape(groups, nodes, cols), mixed))
    me = lax.axis_index("feat")
    order = (2, 3, 1)
    sent = {k: shifted(mixed, k, groups) for k in order}
    blocks = {
        k: lax.dynamic_index_in_dim(feature_blocks, lax.rem(me + groups - k, groups), 0, keepdims=False)
        for k in range(groups)
    }
    blocks |= {k: shifted(blocks[k], k, groups) for k in order}
    blocks = [blocks[k] for k in (0, *order)]
    sent = [sent[k] for k in order]
    sent = [w for a in sent for w in (a, lax.ppermute(a, "dom_2", [(0, 1), (1, 0)]))]

    neigh, own, outgoing = call(
        gather_kernel,
        (hbm((nodes, width), BF16), shape((nodes, width), F32), hbm((chunks, STEP, width), BF16)),
        [VM] * (3 * groups + 2),
        "gather",
        flops=2 * nodes * width * (slots + 2 * groups * cols),
        moved=8 * MIB,
        scratch=[
            buffer((chunks, STEP, nodes), BF16),
            buffer((nodes, width), BF16),
            buffer((chunks, STEP, width), BF16),
            buffer((2, groups - 1, cols, width), BF16),
            sems((chunks,)),
            sems,
        ],
        out_specs=(ANY, VM, ANY),
    )(*blocks, w_neigh, w_self, *sent, targets.T, send_count[0])
    halo = lax.all_to_all(
        outgoing.reshape(parts_total, slot_count, width), FEAT_DOM, split_axis=0, concat_axis=0, tiled=True
    ).reshape(deep, DEEP, width)

    late_src, neigh = lax.optimization_barrier((tile_src[0], neigh))
    near_wide, far_wide, near_tall, far_tall, rdeg = call(
        dense_kernel,
        (
            shape((nodes, nodes), BF16),
            hbm((deep, nodes, DEEP), BF16),
            shape((nodes, nodes), BF16),
            hbm((deep, DEEP, nodes), BF16),
            shape((nodes, size), F32),
        ),
        [SM, SM, SM, ANY],
        "dense",
        flops=16 * nodes * slots,
        moved=16 * MIB,
        scratch=[
            buffer(((nodes + slots) // size * (nodes // size), size, size), F32),
            buffer((tiles, size, size), BF16),
            buffer((deep, nodes, DEEP), BF16),
            buffer((deep, DEEP, nodes), BF16),
            sems((5,)),
            sems((deep,)),
            sems((deep,)),
        ],
        out_specs=(VM, ANY, VM, ANY, VM),
    )(late_src, tile_dst[0], tile_count, far(tile_vals[0, 0]))

    base = call(
        base_kernel,
        hbm((nodes, width), F32),
        [VM] * 4,
        "base",
        flops=2 * nodes * width * (groups * cols + nodes),
        moved=4 * MIB,
    )(own, near_wide, neigh, rdeg)

    pre, sums = call(
        pre_kernel,
        (shape((nodes, width), F32), shape((4, width // 2), F32)),
        [ANY, VM, ANY, VM],
        "pre",
        flops=2 * nodes * width * slots,
        moved=8 * MIB,
        scratch=[buffer((deep, nodes, DEEP), BF16), buffer((nodes, width), F32), sems((deep,)), sems],
    )(far(base), rdeg, far(far_wide), halo)
    sums = exchange_sums(sums, parts_total)

    hidden, slope, normed, scale, grads = call(
        lambda *refs: act_kernel(nodes_total, *refs),
        (
            hbm((nodes, width), BF16),
            shape((nodes, width), F32),
            shape((nodes, width), F32),
            shape((1, width), F32),
            shape((4, width // 2), F32),
        ),
        [VM, VM, VM, VM, ANY],
        "act",
        flops=40 * nodes * width,
        moved=2 * MIB,
        scratch=[buffer((nodes, width), BF16), buffer((nodes, width), BF16), sems((2,))],
        out_specs=(ANY, VM, VM, VM, VM),
    )(pre, sums, gain.reshape(1, width), shift.reshape(1, width), far(d_hidden[0, 0]))
    grads = exchange_sums(grads, parts_total)

    d_self, message, both_grads, leaving = call(
        lambda *refs: back_kernel(nodes_total, *refs),
        (
            hbm((nodes, width), BF16),
            hbm((nodes, width), BF16),
            shape((2, width), F32),
            hbm((deep, DEEP, width), BF16),
        ),
        [VM] * 5 + [ANY],
        "back",
        flops=2 * nodes * width * slots,
        moved=8 * MIB,
        scratch=[
            buffer((deep, DEEP, nodes), BF16),
            buffer((nodes, width), BF16),
            buffer((nodes, width), BF16),
            buffer((deep, DEEP, width), BF16),
            sems((deep,)),
            sems((deep,)),
            sems((2,)),
        ],
        out_specs=(ANY, ANY, VM, ANY),
    )(slope, normed, grads, scale, rdeg, far(far_tall))

    returned = lax.all_to_all(
        leaving.reshape(parts_total, slot_count, width), FEAT_DOM, split_axis=0, concat_axis=0, tiled=True
    ).reshape(deep, DEEP, width)
    late_count, message = lax.optimization_barrier((send_count[0, 0], message))
    live_slot = jnp.arange(slot_count)[None, :] < late_count[:, None]
    chosen = jnp.where(live_slot, targets, -1).reshape(deep, 1, DEEP)
    near = call(
        near_kernel, shape((nodes, width), F32), [VM] * 2, "near", flops=2 * nodes * width * nodes, moved=2 * MIB
    )(near_tall, message)
    d_neigh = call(
        scatter_kernel,
        shape((nodes, width), BF16),
        [VM] * 3,
        "scatter",
        flops=2 * nodes * width * slots,
        moved=8 * MIB,
        scratch=[buffer((nodes, width), F32)],
    )(near, chosen, returned)

    out_shape = (1, 1, nodes, width)
    return (
        hidden.reshape(out_shape),
        d_self.reshape(out_shape),
        d_neigh.reshape(out_shape),
        both_grads[0],
        both_grads[1],
    )


def solution(mesh):
    split = Mesh(
        mesh.devices.reshape(mesh.shape["feat"], 4, 4, 2), ("feat", "dom_0", "dom_1", "dom_2")
    )
    placed = (
        P(None, DOM, None, "feat"),
        P("feat", None),
        P("feat", None),
        P(),
        P(),
        P("feat", DOM, None, None),
        P("feat", DOM, None, None),
        P("feat", DOM, None),
        P("feat", DOM, None),
        P("feat", DOM, None),
        P("feat", DOM),
        P("feat", DOM, None, None, None),
    )
    return jax.shard_map(
        shards,
        mesh=split,
        in_specs=placed,
        out_specs=(
            P("feat", DOM, None, None),
            P("feat", DOM, None, None),
            P("feat", DOM, None, None),
            P(),
            P(),
        ),
        check_vma=False,
    )
```

```python
import jax
import jax.numpy as jnp
from jax import lax
from jax.experimental import pallas as pl
from jax.experimental.pallas import tpu as pltpu
from jax.sharding import Mesh
from jax.sharding import PartitionSpec as P

FEAT_DOM = ("feat", "dom_0", "dom_1", "dom_2")
DOM = ("dom_0", "dom_1", "dom_2")
EPSILON = 1e-05
F32 = jnp.float32
BF16 = jnp.bfloat16
MIB = 1 << 20

VM = pl.BlockSpec(memory_space=pltpu.VMEM)
SM = pl.BlockSpec(memory_space=pltpu.SMEM)
ANY = pl.BlockSpec(memory_space=pl.ANY)
STEP = 512
DEEP = 1024


def far(x):
    return pltpu.with_memory_space_constraint(x, pltpu.HBM)


def call(body, outs, ins, name, flops=0, moved=0, scratch=(), limit=40, out_specs=None):
    return pl.pallas_call(
        body,
        out_shape=outs,
        in_specs=ins,
        out_specs=out_specs if out_specs is not None else jax.tree.map(lambda _: VM, outs),
        scratch_shapes=list(scratch),
        name=name,
        compiler_params=pltpu.CompilerParams(vmem_limit_bytes=limit * MIB),
        cost_estimate=pl.CostEstimate(flops=flops, bytes_accessed=moved, transcendentals=0),
    )


def pieces(source, target, sems, each=1):
    count = source.shape[0] // each
    return [
        pltpu.make_async_copy(
            source.at[pl.ds(c * each, each)], target.at[pl.ds(c * each, each)], sems.at[c]
        )
        for c in range(count)
    ]


def dot(a, b):
    return jnp.dot(a, b, preferred_element_type=F32)


def dense_kernel(
    src_ref, dst_ref, count_ref, vals_hbm,
    al_ref, ah_hbm, tl_ref, th_hbm, rdeg_ref,
    acc_ref, vals_ref, wide_ref, tall_ref, in_sem, wide_sem, tall_sem,
):
    size = vals_ref.shape[1]
    blocks = al_ref.shape[0] // size
    chunks = wide_ref.shape[0]
    per_chunk = wide_ref.shape[2] // size
    parts = in_sem.shape[0]
    tiles = vals_ref.shape[0] // parts

    def arriving(c):
        at = pl.ds(c * tiles, tiles)
        return pltpu.make_async_copy(vals_hbm.at[at], vals_ref.at[at], in_sem.at[c])

    for c in range(parts):
        arriving(c).start()

    def clear(i, carry):
        for b in range(blocks):
            acc_ref[i * blocks + b] = jnp.zeros((size, size), F32)
        return carry

    lax.fori_loop(0, acc_ref.shape[0] // blocks, clear, 0)

    def add(t, carry):
        at = src_ref[0, t] * blocks + dst_ref[0, t]
        acc_ref[at] += vals_ref[t].astype(F32)
        return carry

    live = count_ref[0, 0]
    for c in range(parts):
        arriving(c).wait()
        lax.fori_loop(jnp.minimum(c * tiles, live), jnp.minimum((c + 1) * tiles, live), add, 0)

    rdeg_ref[...] = jnp.zeros(rdeg_ref.shape, F32)

    def place(s, put_wide, put_tall, at):
        for b in range(blocks):
            rows = slice(b * size, (b + 1) * size)
            tile = acc_ref[s * blocks + b]
            rdeg_ref[rows, :] += tile
            put_wide[rows, at * size : (at + 1) * size] = tile.astype(BF16)
            put_tall[at * size : (at + 1) * size, rows] = tile.T.astype(BF16)

    for s in range(blocks):
        place(s, al_ref, tl_ref, s)

    far_out = pieces(wide_ref, ah_hbm, wide_sem) + pieces(tall_ref, th_hbm, tall_sem)
    tall_per = tall_ref.shape[1] // size
    for s in range(chunks * per_chunk):
        place(
            blocks + s,
            wide_ref.at[s // per_chunk, :, pl.ds(s % per_chunk * size, size)],
            tall_ref.at[s // tall_per, pl.ds(s % tall_per * size, size), :],
            0,
        )
        if s % per_chunk == per_chunk - 1:
            far_out[s // per_chunk].start()
        if s % tall_per == tall_per - 1:
            far_out[chunks + s // tall_per].start()

    for b in range(blocks):
        rows = pl.ds(b * size, size)
        total = 1.0 + jnp.sum(rdeg_ref[rows, :], axis=1, keepdims=True)
        rdeg_ref[rows, :] = jnp.broadcast_to(1.0 / total, (size, size))
    for copy in far_out:
        copy.wait()


def projected(blocks, mine_ref, sent, weight_ref, which):
    half = mine_ref.shape[0] // 2
    core = lax.axis_index("dom_2")
    near = pl.ds(pl.multiple_of(core * half, half), half)
    far = pl.ds(pl.multiple_of((1 - core) * half, half), half)
    rows = slice(which * half, (which + 1) * half)
    total = dot(blocks[0][...], mine_ref[...])
    for k, (a, b) in enumerate(sent):
        weight_ref[k, near, :] = a[rows, :]
        weight_ref[k, far, :] = b[rows, :]
        total += dot(blocks[k + 1][...], weight_ref[k])
    return total


def gather_kernel(
    f0_ref, f1_ref, f2_ref, f3_ref, neigh_w_ref, self_w_ref, a1_ref, b1_ref, a2_ref, b2_ref, a3_ref, b3_ref,
    rows_ref, count_ref, neigh_hbm, own_ref, out_hbm, tall_ref, neigh_ref, out_ref, weight_ref, out_sem, neigh_sem,
):
    blocks = (f0_ref, f1_ref, f2_ref, f3_ref)
    sent = ((a1_ref, b1_ref), (a2_ref, b2_ref), (a3_ref, b3_ref))
    slot_count = rows_ref.shape[0]
    chunks, step, nodes = tall_ref.shape
    per_chunk = step // slot_count
    leaving = pieces(out_ref, out_hbm, out_sem)
    order = lax.broadcasted_iota(jnp.int32, rows_ref.shape, 0)
    chosen = jnp.where(order < count_ref[...], rows_ref[...], -1)
    along = lax.broadcasted_iota(jnp.int32, (slot_count, nodes), 1)
    neigh_ref[...] = projected(blocks, neigh_w_ref, sent, weight_ref.at[0], 0).astype(BF16)
    keep = pltpu.make_async_copy(neigh_ref, neigh_hbm, neigh_sem)
    keep.start()
    for c, go in enumerate(leaving):
        for k in range(per_chunk):
            q = c * per_chunk + k
            hot = jnp.where(along == chosen[:, q : q + 1], 1.0, 0.0).astype(BF16)
            tall_ref[c, k * slot_count : (k + 1) * slot_count, :] = hot
        out_ref[c] = dot(tall_ref[c], neigh_ref[...]).astype(BF16)
        go.start()
    own_ref[...] = projected(blocks, self_w_ref, sent, weight_ref.at[1], 1)
    for copy in leaving:
        copy.wait()
    keep.wait()


def both_halves(rdeg):
    return jnp.concatenate([rdeg, rdeg], axis=1)


def base_kernel(own_ref, al_ref, neigh_ref, rdeg_ref, base_ref):
    base_ref[...] = own_ref[...] + dot(al_ref[...], neigh_ref[...]) * both_halves(rdeg_ref[...])


def put_sums(ref, first, second):
    half = ref.shape[1]
    ref[0:1, :] = first[:, :half]
    ref[1:2, :] = first[:, half:]
    ref[2:3, :] = second[:, :half]
    ref[3:4, :] = second[:, half:]


def get_sums(ref):
    first = jnp.concatenate([ref[0:1, :], ref[1:2, :]], axis=1)
    second = jnp.concatenate([ref[2:3, :], ref[3:4, :]], axis=1)
    return first, second


def pre_kernel(base_hbm, rdeg_ref, ah_hbm, halo_ref, pre_ref, sums_ref, ah_ref, base_ref, sems, base_sem):
    arriving = pieces(ah_hbm, ah_ref, sems)
    for copy in arriving:
        copy.start()
    late = pltpu.make_async_copy(base_hbm, base_ref, base_sem)
    late.start()
    for c, come in enumerate(arriving):
        come.wait()
        term = dot(ah_ref[c], halo_ref[c])
        if c == 0:
            pre_ref[...] = term
        elif c < len(arriving) - 1:
            pre_ref[...] += term
    late.wait()
    pre = base_ref[...] + (pre_ref[...] + term) * both_halves(rdeg_ref[...])
    pre_ref[...] = pre
    put_sums(sums_ref, jnp.sum(pre, axis=0, keepdims=True), jnp.sum(pre * pre, axis=0, keepdims=True))


def act_kernel(
    nodes_total, pre_ref, sums_ref, gain_ref, shift_ref, cot_hbm,
    hidden_hbm, slope_ref, normed_ref, scale_ref, out_ref, cot_ref, hidden_ref, sems,
):
    come = pltpu.make_async_copy(cot_hbm, cot_ref, sems.at[0])
    go = pltpu.make_async_copy(hidden_ref, hidden_hbm, sems.at[1])
    come.start()
    column, squares = get_sums(sums_ref)
    mean = column / nodes_total
    variance = squares / nodes_total - mean * mean
    inverse = 1.0 / jnp.sqrt(variance + EPSILON)
    scale_ref[...] = gain_ref[...] * inverse
    normed = (pre_ref[...] - mean) * inverse
    act = gain_ref[...] * normed + shift_ref[...]
    logistic = 1.0 / (1.0 + jnp.exp(-act))
    hidden_ref[...] = (act * logistic).astype(BF16)
    normed_ref[...] = normed
    slope_ref[...] = logistic * (1.0 + act * (1.0 - logistic))
    go.start()
    come.wait()
    slope = cot_ref[...].astype(F32) * slope_ref[...]
    slope_ref[...] = slope
    put_sums(
        out_ref, jnp.sum(slope, axis=0, keepdims=True), jnp.sum(slope * normed_ref[...], axis=0, keepdims=True)
    )
    go.wait()


def back_kernel(
    nodes_total, slope_ref, normed_ref, sums_ref, scale_ref, rdeg_ref, th_hbm,
    dself_hbm, message_hbm, grads_ref, out_hbm, th_ref, dself_ref, message_ref, out_ref, in_sem, out_sem, keep_sem,
):
    arriving = pieces(th_hbm, th_ref, in_sem)
    leaving = pieces(out_ref, out_hbm, out_sem)
    keeping = [
        pltpu.make_async_copy(dself_ref, dself_hbm, keep_sem.at[0]),
        pltpu.make_async_copy(message_ref, message_hbm, keep_sem.at[1]),
    ]
    half = len(arriving) // 2
    for copy in arriving[:half]:
        copy.start()
    first, second = get_sums(sums_ref)
    shift_grad = first / nodes_total
    gain_grad = second / nodes_total
    grads_ref[0:1, :] = gain_grad
    grads_ref[1:2, :] = shift_grad
    dpre = scale_ref[...] * (slope_ref[...] - shift_grad - normed_ref[...] * gain_grad)
    dself_ref[...] = dpre.astype(BF16)
    message_ref[...] = (dpre * both_halves(rdeg_ref[...])).astype(BF16)
    for copy in arriving[half:]:
        copy.start()
    for c, go in enumerate(leaving):
        if c % half == 0:
            for come in arriving[c : c + half]:
                come.wait()
        out_ref[c] = dot(th_ref[c], message_ref[...]).astype(BF16)
        go.start()
        if c == half:
            for copy in keeping:
                copy.start()
    for copy in leaving + keeping:
        copy.wait()


def near_kernel(tl_ref, message_ref, out_ref):
    out_ref[...] = dot(tl_ref[...], message_ref[...])


def scatter_kernel(near_ref, row_ref, back_ref, out_ref, acc_ref):
    deep, step, _ = back_ref.shape
    nodes = out_ref.shape[0]
    down = lax.broadcasted_iota(jnp.int32, (nodes, step), 0)
    acc_ref[...] = near_ref[...]
    for c in range(deep):
        wide = jnp.where(down == row_ref[c], 1.0, 0.0).astype(BF16)
        acc_ref[...] += dot(wide, back_ref[c])
    out_ref[...] = acc_ref[...].astype(BF16)


def exchange_sums(sums, devices):
    spread = jnp.broadcast_to(sums[None], (devices,) + sums.shape)
    return jnp.sum(lax.all_to_all(spread, FEAT_DOM, split_axis=0, concat_axis=0, tiled=True), axis=0)


def shifted(array, k, groups):
    return lax.ppermute(array, "feat", [((j + k) % groups, j) for j in range(groups)])


def shards(
    features,
    w_self,
    w_neigh,
    gain,
    shift,
    d_hidden,
    send_rows,
    send_count,
    tile_src,
    tile_dst,
    tile_count,
    tile_vals,
):
    groups, _, nodes, cols = features.shape
    width = w_self.shape[1]
    tiles, size = tile_vals.shape[2:4]
    targets = send_rows[0, 0]
    parts_total, slot_count = targets.shape
    slots = parts_total * slot_count
    chunks = slots // STEP
    nodes_total = float(nodes * parts_total)
    deep = slots // DEEP
    shape = jax.ShapeDtypeStruct
    hbm = pltpu.HBM
    buffer = pltpu.VMEM
    sems = pltpu.SemaphoreType.DMA

    core_half = cols // 2
    start = lax.axis_index("dom_2") * core_half
    mixed = jnp.concatenate(
        [lax.dynamic_slice_in_dim(w, start, core_half, 0) for w in (w_neigh, w_self)], axis=0
    )
    feature_blocks, mixed = lax.optimization_barrier((features.reshape(groups, nodes, cols), mixed))
    me = lax.axis_index("feat")
    order = (3, 1, 2)
    sent = {k: shifted(mixed, k, groups) for k in order}
    blocks = {
        k: lax.dynamic_index_in_dim(feature_blocks, lax.rem(me + groups - k, groups), 0, keepdims=False)
        for k in range(groups)
    }
    blocks |= {k: shifted(blocks[k], k, groups) for k in order}
    blocks = [blocks[k] for k in (0, *order)]
    sent = [sent[k] for k in order]
    sent = [w for a in sent for w in (a, lax.ppermute(a, "dom_2", [(0, 1), (1, 0)]))]

    neigh, own, outgoing = call(
        gather_kernel,
        (hbm((nodes, width), BF16), shape((nodes, width), F32), hbm((chunks, STEP, width), BF16)),
        [VM] * (3 * groups + 2),
        "gather",
        flops=2 * nodes * width * (slots + 2 * groups * cols),
        moved=8 * MIB,
        scratch=[
            buffer((chunks, STEP, nodes), BF16),
            buffer((nodes, width), BF16),
            buffer((chunks, STEP, width), BF16),
            buffer((2, groups - 1, cols, width), BF16),
            sems((chunks,)),
            sems,
        ],
        out_specs=(ANY, VM, ANY),
    )(*blocks, w_neigh, w_self, *sent, targets.T, send_count[0])
    halo = lax.all_to_all(
        outgoing.reshape(parts_total, slot_count, width), FEAT_DOM, split_axis=0, concat_axis=0, tiled=True
    ).reshape(deep, DEEP, width)

    late_src, neigh = lax.optimization_barrier((tile_src[0], neigh))
    near_wide, far_wide, near_tall, far_tall, rdeg = call(
        dense_kernel,
        (
            shape((nodes, nodes), BF16),
            hbm((deep, nodes, DEEP), BF16),
            shape((nodes, nodes), BF16),
            hbm((deep, DEEP, nodes), BF16),
            shape((nodes, size), F32),
        ),
        [SM, SM, SM, ANY],
        "dense",
        flops=16 * nodes * slots,
        moved=16 * MIB,
        scratch=[
            buffer(((nodes + slots) // size * (nodes // size), size, size), F32),
            buffer((tiles, size, size), BF16),
            buffer((deep, nodes, DEEP), BF16),
            buffer((deep, DEEP, nodes), BF16),
            sems((5,)),
            sems((deep,)),
            sems((deep,)),
        ],
        out_specs=(VM, ANY, VM, ANY, VM),
    )(late_src, tile_dst[0], tile_count, far(tile_vals[0, 0]))

    base = call(
        base_kernel,
        hbm((nodes, width), F32),
        [VM] * 4,
        "base",
        flops=2 * nodes * width * (groups * cols + nodes),
        moved=4 * MIB,
    )(own, near_wide, neigh, rdeg)

    pre, sums = call(
        pre_kernel,
        (shape((nodes, width), F32), shape((4, width // 2), F32)),
        [ANY, VM, ANY, VM],
        "pre",
        flops=2 * nodes * width * slots,
        moved=8 * MIB,
        scratch=[buffer((deep, nodes, DEEP), BF16), buffer((nodes, width), F32), sems((deep,)), sems],
    )(far(base), rdeg, far(far_wide), halo)
    sums = exchange_sums(sums, parts_total)

    hidden, slope, normed, scale, grads = call(
        lambda *refs: act_kernel(nodes_total, *refs),
        (
            hbm((nodes, width), BF16),
            shape((nodes, width), F32),
            shape((nodes, width), F32),
            shape((1, width), F32),
            shape((4, width // 2), F32),
        ),
        [VM, VM, VM, VM, ANY],
        "act",
        flops=40 * nodes * width,
        moved=2 * MIB,
        scratch=[buffer((nodes, width), BF16), buffer((nodes, width), BF16), sems((2,))],
        out_specs=(ANY, VM, VM, VM, VM),
    )(pre, sums, gain.reshape(1, width), shift.reshape(1, width), far(d_hidden[0, 0]))
    grads = exchange_sums(grads, parts_total)

    d_self, message, both_grads, leaving = call(
        lambda *refs: back_kernel(nodes_total, *refs),
        (
            hbm((nodes, width), BF16),
            hbm((nodes, width), BF16),
            shape((2, width), F32),
            hbm((deep, DEEP, width), BF16),
        ),
        [VM] * 5 + [ANY],
        "back",
        flops=2 * nodes * width * slots,
        moved=8 * MIB,
        scratch=[
            buffer((deep, DEEP, nodes), BF16),
            buffer((nodes, width), BF16),
            buffer((nodes, width), BF16),
            buffer((deep, DEEP, width), BF16),
            sems((deep,)),
            sems((deep,)),
            sems((2,)),
        ],
        out_specs=(ANY, ANY, VM, ANY),
    )(slope, normed, grads, scale, rdeg, far(far_tall))

    returned = lax.all_to_all(
        leaving.reshape(parts_total, slot_count, width), FEAT_DOM, split_axis=0, concat_axis=0, tiled=True
    ).reshape(deep, DEEP, width)
    late_count, message = lax.optimization_barrier((send_count[0, 0], message))
    live_slot = jnp.arange(slot_count)[None, :] < late_count[:, None]
    chosen = jnp.where(live_slot, targets, -1).reshape(deep, 1, DEEP)
    near = call(
        near_kernel, shape((nodes, width), F32), [VM] * 2, "near", flops=2 * nodes * width * nodes, moved=2 * MIB
    )(near_tall, message)
    d_neigh = call(
        scatter_kernel,
        shape((nodes, width), BF16),
        [VM] * 3,
        "scatter",
        flops=2 * nodes * width * slots,
        moved=8 * MIB,
        scratch=[buffer((nodes, width), F32)],
    )(near, chosen, returned)

    out_shape = (1, 1, nodes, width)
    return (
        hidden.reshape(out_shape),
        d_self.reshape(out_shape),
        d_neigh.reshape(out_shape),
        both_grads[0],
        both_grads[1],
    )


def solution(mesh):
    split = Mesh(
        mesh.devices.reshape(mesh.shape["feat"], 4, 4, 2), ("feat", "dom_0", "dom_1", "dom_2")
    )
    placed = (
        P(None, DOM, None, "feat"),
        P("feat", None),
        P("feat", None),
        P(),
        P(),
        P("feat", DOM, None, None),
        P("feat", DOM, None, None),
        P("feat", DOM, None),
        P("feat", DOM, None),
        P("feat", DOM, None),
        P("feat", DOM),
        P("feat", DOM, None, None, None),
    )
    return jax.shard_map(
        shards,
        mesh=split,
        in_specs=placed,
        out_specs=(
            P("feat", DOM, None, None),
            P("feat", DOM, None, None),
            P("feat", DOM, None, None),
            P(),
            P(),
        ),
        check_vma=False,
    )
```
